32 devices in a mesh: dp: 8 (over y, x, core), ctx: 4 (over z).
Axes of the slice: x: 2, y: 2, z: 4, core: 2. Of those that a mesh axis runs over, the one named last changes fastest.
Arguments:
- query_frames: bfloat16 [8192, 2560], P(('dp', 'ctx')), parts along dimension 0, may hold values from -8 to 8
- key_frames: bfloat16 [8192, 2560], P(('dp', 'ctx')), parts along dimension 0, may hold values from -8 to 8
- value_frames: bfloat16 [8192, 2560], P(('dp', 'ctx')), parts along dimension 0, may hold values from -6 to 6
- stream: bfloat16 [8192, 5120], P(('dp', 'ctx')), parts along dimension 0, may hold values from -1.25 to 1.25
- out_weight: bfloat16 [2560, 5120], P('ctx'), may hold values from -0.125 to 0.125
Outputs:
- layer_out: bfloat16 [8192, 5120], P(('dp', 'ctx')), parts along dimension 0
The draws below stay inside these ranges and needn't reach their ends.
There are 8 independent parts, one for each index of `dp`. The reference program is written for one: setup_inputs(seed, part) draws one part's arguments, and reference() takes and returns one part's arrays. A program takes and returns all parts, laid end to end along the dimension named above; an argument that names none is the same for every part. Nothing has to cross between parts.
All inputs are finite; a program needn't handle non-finite values.
Results may differ from the reference program's by a relative error of at most 0.01.
Values may be sent and summed in bfloat16 or wider, within the bound.
No kernel may reach another device: no remote copies, remote signals or barrier semaphores. Data moves between devices by JAX's collectives and lax.ppermute only.
A program may use at most 128 MiB of HBM per device.

```python
import jax
import jax.numpy as jnp
from jax import lax

D = 5120
HEADS = 20
HEAD_SIZE = 128
TOK_DEV = 256
TOKENS = 1024


def draw_query_frames(key, part):
    result = jnp.clip(jax.random.normal(jax.random.fold_in(key, 1), (TOKENS, HEADS * HEAD_SIZE), jnp.float32), -6.0, 6.0)
    return result.astype(jnp.bfloat16)


def draw_key_frames(key, part):
    result = jnp.clip(jax.random.normal(jax.random.fold_in(key, 2), (TOKENS, HEADS * HEAD_SIZE), jnp.float32), -6.0, 6.0)
    return result.astype(jnp.bfloat16)


def shard_levels(rng, dims, shards, low, high):
    def one(axis_at, parts):
        draws = jax.random.uniform(jax.random.fold_in(jax.random.fold_in(rng, 6), axis_at), (parts,), jnp.float32, low / len(shards), high / len(shards))
        return jnp.repeat(jnp.exp(draws), dims[axis_at] // parts).reshape((-1,) + (1,) * (len(dims) - axis_at - 1))

    factor_of = one(*shards[0])
    for cut in shards[1:]:
        factor_of = factor_of * one(*cut)
    return factor_of


def centred(stream_key, shape, width, most, pieces=(), kind=jnp.bfloat16):
    gain = shard_levels(stream_key, shape, pieces, -0.22, 0.18) if pieces else 1.0
    drawn = jax.random.normal(stream_key, shape, jnp.float32) * width * gain
    return jnp.minimum(jnp.maximum(drawn, -most), most).astype(kind)


def setup_inputs(seed: int = 0, part: int = 0) -> dict:
    seeds = jax.random.split(jax.random.key(seed), 6)
    part_splits = jax.random.split(jax.random.fold_in(seeds[5], part), 6)
    query_frames = draw_query_frames(jax.random.fold_in(jax.random.fold_in(seeds[5], part), 71), part)
    key_frames = draw_key_frames(jax.random.fold_in(jax.random.fold_in(seeds[5], part), 71), part)
    value_frames = centred(part_splits[2], (TOKENS, HEADS * HEAD_SIZE), 1.0, 6.0, ((0, 4),))
    stream = centred(part_splits[3], (TOKENS, D), 0.08, 1.25, ((0, 4),))
    out_weight = centred(seeds[4], (HEADS * HEAD_SIZE, D), (HEADS * HEAD_SIZE) ** -0.5, 0.125, ((0, 4),))
    return dict(query_frames=query_frames, key_frames=key_frames, value_frames=value_frames, stream=stream, out_weight=out_weight)


def attend_block(blocks):
    query_block, key_window, value_window, block_index = blocks
    count = TOKENS // TOK_DEV
    earlier_ok = jnp.broadcast_to(block_index > 0, (TOK_DEV,))
    middle_ok = jnp.ones((TOK_DEV,), dtype=bool)
    later_ok = jnp.broadcast_to(block_index < count - 1, (TOK_DEV,))
    valid = jnp.concatenate([earlier_ok, middle_ok, later_ok])
    scores = jnp.einsum("qhd,khd->hqk", query_block.astype(jnp.float32), key_window.astype(jnp.float32)) * (HEAD_SIZE ** -0.5)
    scores = jnp.where(valid[None, None, :], scores, -1e30)
    largest = jnp.max(scores, axis=2, keepdims=True)
    expon = jnp.exp(scores - largest)
    probs = (expon / jnp.sum(expon, axis=2, keepdims=True)).astype(jnp.bfloat16)
    context = jnp.einsum("hqk,khd->qhd", probs.astype(jnp.float32), value_window.astype(jnp.float32))
    return context.astype(jnp.bfloat16).reshape(TOK_DEV, HEADS * HEAD_SIZE)


def reference(query_frames, key_frames, value_frames, stream, out_weight):
    blocks = TOKENS // TOK_DEV
    query_blocks = query_frames.reshape(blocks, TOK_DEV, HEADS, HEAD_SIZE)
    key_blocks = key_frames.reshape(blocks, TOK_DEV, HEADS, HEAD_SIZE)
    value_blocks = value_frames.reshape(blocks, TOK_DEV, HEADS, HEAD_SIZE)
    key_window = jnp.concatenate([jnp.roll(key_blocks, 1, axis=0), key_blocks, jnp.roll(key_blocks, -1, axis=0)], axis=1)
    value_window = jnp.concatenate([jnp.roll(value_blocks, 1, axis=0), value_blocks, jnp.roll(value_blocks, -1, axis=0)], axis=1)
    block_ids = jnp.arange(blocks, dtype=jnp.int32)
    context = lax.map(attend_block, (query_blocks, key_window, value_window, block_ids)).reshape(TOKENS, HEADS * HEAD_SIZE)
    product = jnp.dot(context, out_weight, preferred_element_type=jnp.float32)
    return (stream.astype(jnp.float32) + product).astype(jnp.bfloat16)
```

```python
import functools

import jax
import jax.numpy as jnp
from jax import lax
from jax.experimental import pallas as pl
from jax.experimental.pallas import tpu as pltpu
from jax.sharding import PartitionSpec as P

HEAD_SIZE = 128
LOG2_E = 1.4426950408889634
LOW = -1e30
MIB = 1024 * 1024


def passed_along(value, steps):
    count = lax.axis_size("ctx")
    leading, last = (max(0, -steps), min(count, count - steps))
    return lax.ppermute(value, "ctx", [(source, source + steps) for source in range(leading, last)])


def passed_round(value):
    count = lax.axis_size("ctx")
    return lax.ppermute(value, "ctx", [(source, (source + 1) % count) for source in range(count)])


def swapped(value, mask):
    count = lax.axis_size("dp")
    return lax.ppermute(value, "dp", [(source, source ^ mask) for source in range(count)])


def after(value, *tokens):
    def kernel(*refs):
        del refs

    place = pl.BlockSpec(memory_space=pl.ANY)
    return pl.pallas_call(
        kernel,
        out_shape=jax.ShapeDtypeStruct(value.shape, value.dtype),
        in_specs=[place] * (1 + len(tokens)),
        out_specs=place,
        input_output_aliases={0: 0},
        cost_estimate=pl.CostEstimate(flops=0, bytes_accessed=0, transcendentals=0),
        name="after",
    )(value, *tokens)


def near(piece):
    count = lax.axis_size("dp")
    return {1 << at: [swapped(piece, 1 << at)] for at in range(1, count.bit_length() - 1)}


def far(pieces):
    count = lax.axis_size("dp")
    pieces = dict(pieces)
    for mask in range(2, count, 2):
        if mask in pieces:
            continue
        low = mask & -mask
        high = mask ^ low
        if high & (high - 1) == 0:
            half = pieces[low][0].shape[0] // 2
            pieces[mask] = [swapped(pieces[low][0][:half], high), swapped(pieces[high][0][half:], low)]
        else:
            pieces[mask] = [swapped(part, low) for part in pieces[high]]
    return pieces


def both_cores(pieces):
    count = lax.axis_size("dp")
    pieces = dict(pieces)
    for mask in range(0, count, 2):
        pieces[mask ^ 1] = [swapped(part, 1) for part in pieces[mask]]
    return [pieces[mask] for mask in range(count)]


def pack_kernel(groups, key_up, value_up, key_down, value_down, token_ref, up_ref, down_ref):
    rows = key_up.shape[0]
    up_ref[:rows] = key_up[...]
    up_ref[rows:] = value_up[...]
    down_ref[:rows] = key_down[...]
    down_ref[rows:] = value_down[...]


def packed(groups, key_frames, value_frames, token, width):
    rows = key_frames.shape[0]
    shape = jax.ShapeDtypeStruct((2 * rows, width), key_frames.dtype)
    up = pl.BlockSpec((rows, width), lambda step, groups: (0, groups[0]))
    down = pl.BlockSpec((rows, width), lambda step, groups: (0, groups[1]))
    both = pl.BlockSpec((2 * rows, width), lambda step, groups: (0, 0))
    return pl.pallas_call(
        pack_kernel,
        out_shape=(shape, shape),
        grid_spec=pltpu.PrefetchScalarGridSpec(
            num_scalar_prefetch=1,
            grid=(1,),
            in_specs=[up, up, down, down, pl.BlockSpec(memory_space=pl.ANY)],
            out_specs=[both, both],
        ),
        compiler_params=pltpu.CompilerParams(vmem_limit_bytes=16 * MIB),
        cost_estimate=pl.CostEstimate(flops=0, bytes_accessed=8 * rows * width * 2, transcendentals=0),
        name="pack_window",
    )(groups, key_frames, value_frames, key_frames, value_frames, token)


def attend_kernel(place, query_ref, key_ref, value_ref, earlier_ref, later_ref, context_ref):
    rows, width = query_ref.shape
    ones = jnp.ones((rows, HEAD_SIZE), jnp.bfloat16)
    sides = ((earlier_ref, place[1] > 0), (later_ref, place[2] > 0))
    for at in range(0, width, HEAD_SIZE):
        head = pl.ds(at, HEAD_SIZE)
        query = query_ref[:, head]

        def scores(keys):
            return lax.dot_general(query, keys, (((1,), (1,)), ((), ())), preferred_element_type=jnp.float32)

        parts = [scores(key_ref[:, head])]
        values = [value_ref[:, head]]
        for side, there in sides:
            parts.append(jnp.where(there, scores(side[:rows, head]), LOW))
            values.append(side[rows:, head])
        largest = jnp.max(functools.reduce(jnp.maximum, parts), axis=1, keepdims=True)
        sums = 0.0
        for part, value in zip(parts, values):
            expon = jnp.exp2((part - largest) * (HEAD_SIZE ** (-0.5) * LOG2_E)).astype(jnp.bfloat16)
            sums += jnp.dot(expon, jnp.concatenate([value, ones], 1), preferred_element_type=jnp.float32)
        context_ref[:, head] = (sums[:, :HEAD_SIZE] / sums[:, HEAD_SIZE:]).astype(context_ref.dtype)


def attended(place, query_frames, key_frames, value_frames, earlier, later):
    rows, width = earlier.shape[0] // 2, earlier.shape[1]
    heads = width // HEAD_SIZE
    own = pl.BlockSpec((rows, width), lambda step, place: (0, place[0]))
    other = pl.BlockSpec((2 * rows, width), lambda step, place: (0, 0))
    return pl.pallas_call(
        attend_kernel,
        out_shape=jax.ShapeDtypeStruct((rows, width), query_frames.dtype),
        grid_spec=pltpu.PrefetchScalarGridSpec(
            num_scalar_prefetch=1,
            grid=(1,),
            in_specs=[own, own, own, other, other],
            out_specs=pl.BlockSpec((rows, width), lambda step, place: (0, 0)),
        ),
        compiler_params=pltpu.CompilerParams(vmem_limit_bytes=24 * MIB),
        cost_estimate=pl.CostEstimate(
            flops=12 * rows * rows * width,
            bytes_accessed=16 * rows * width,
            transcendentals=3 * rows * rows * heads,
        ),
        name="attend_heads",
    )(place, query_frames, key_frames, value_frames, earlier, later)


def project_kernel(counts, blocks, own, *refs):
    step = pl.program_id(0)
    context_refs, refs = refs[: len(counts) + own], refs[len(counts) + own :]
    if own:
        weight_ref, refs = refs[0], refs[1:]
    base_ref, refs = refs[0], refs[1:]
    pieces = []
    for count in counts:
        slot = []
        for parts in count:
            slot.append(refs[:parts])
            refs = refs[parts:]
        pieces.append(slot)
    out_ref, held, sems = refs

    @pl.when(step == 0)
    def _():
        for block in range(blocks):
            for slot, parts_of in enumerate(pieces):
                at = 0
                for part in parts_of[block]:
                    pltpu.make_async_copy(
                        part, held.at[slot, block, pl.ds(at, part.shape[0])], sems.at[slot, block]
                    ).start()
                    at += part.shape[0]

    result = base_ref[...].astype(jnp.float32)
    if own:
        result += jnp.dot(context_refs[0][...], weight_ref[...], preferred_element_type=jnp.float32)
    for slot in range(len(counts)):
        whole = held.at[slot, step]
        pltpu.make_async_copy(whole, whole, sems.at[slot, step]).wait()
        result += jnp.dot(context_refs[slot + own][...], whole[...], preferred_element_type=jnp.float32)
    out_ref[...] = result.astype(out_ref.dtype)


def projected(place, contexts, weight, slots, base, out_dtype):
    rows, depth = contexts[0].shape
    blocks = len(slots[0])
    columns = base.shape[1] // blocks
    own = int(weight is not None)
    counts = tuple(tuple(len(parts) for parts in slot) for slot in slots)
    flat = [part for slot in slots for parts in slot for part in parts]
    column = lambda step, place: (0, lax.bitwise_xor(place[0], step))

    def kernel(place, *refs):
        project_kernel(counts, blocks, own, *refs)

    size = len(contexts) * depth * base.shape[1]
    return pl.pallas_call(
        kernel,
        out_shape=jax.ShapeDtypeStruct(base.shape, out_dtype),
        grid_spec=pltpu.PrefetchScalarGridSpec(
            num_scalar_prefetch=1,
            grid=(blocks,),
            in_specs=[pl.BlockSpec((rows, depth), lambda step, place: (0, 0)) for _ in contexts]
            + [pl.BlockSpec((depth, columns), column)] * own
            + [pl.BlockSpec((rows, columns), column)]
            + [pl.BlockSpec(memory_space=pl.ANY)] * len(flat),
            out_specs=pl.BlockSpec((rows, columns), column),
            scratch_shapes=[
                pltpu.VMEM((len(slots), blocks, depth, columns), jnp.bfloat16),
                pltpu.SemaphoreType.DMA((len(slots), blocks)),
            ],
        ),
        compiler_params=pltpu.CompilerParams(vmem_limit_bytes=32 * MIB),
        cost_estimate=pl.CostEstimate(
            flops=2 * rows * size,
            bytes_accessed=2 * size + 8 * rows * base.shape[1],
            transcendentals=0,
        ),
        name="project_slots",
    )(place, *contexts, *([weight] * own), base, *flat)


def by_slots(query_frames, key_frames, value_frames, stream, out_weight):
    width, columns = out_weight.shape
    position, members = lax.axis_index("ctx"), lax.axis_size("ctx")
    lane, lanes = lax.axis_index("dp"), lax.axis_size("dp")
    lane_place = jnp.stack([lane]).astype(jnp.int32)

    def group(slot):
        return lax.rem(position - slot + 2 * members, members)

    share = columns // lanes
    moving = lax.dynamic_slice_in_dim(out_weight, lane * share, share, 1)
    arrived, beside = [], []
    for slot in range(1, members):
        moving = passed_round(moving)
        if beside:
            moving = after(moving, *[part for parts in beside[-1].values() for part in parts])
        arrived.append(moving)
        beside.append(near(moving))
    slots = [both_cores(far({0: [piece], **pieces})) for piece, pieces in zip(arrived, beside)]

    contexts = []
    for slot in range(members):
        groups = jnp.stack([group(slot - 1), group(slot + 1)]).astype(jnp.int32)
        up, down = packed(groups, key_frames, value_frames, arrived[min(slot + 1, members - 2)], width)
        earlier, later = passed_along(up, 1), passed_along(down, -1)
        place = jnp.stack([group(slot), position, members - 1 - position]).astype(jnp.int32)
        contexts.append(attended(place, query_frames, key_frames, value_frames, earlier, later))

    sums = projected(lane_place, contexts[:-1], out_weight, slots[:-1], stream, jnp.float32)
    return projected(lane_place, contexts[-1:], None, slots[-1:], sums, stream.dtype)


def whole_window(query_frames, key_frames, value_frames, stream, out_weight):
    rows, width = query_frames.shape
    heads = width // HEAD_SIZE
    position, members = lax.axis_index("ctx"), lax.axis_size("ctx")
    both = jnp.stack([key_frames, value_frames], 0)
    window = jnp.concatenate([passed_along(both, 1), both, passed_along(both, -1)], 1)
    valid = jnp.repeat(jnp.stack([position > 0, True, position < members - 1]), rows)
    query, key, value = (a.reshape(-1, heads, HEAD_SIZE) for a in (query_frames, window[0], window[1]))
    scores = jnp.einsum("qhd,khd->hqk", query, key, preferred_element_type=jnp.float32) * HEAD_SIZE ** (-0.5)
    probs = jax.nn.softmax(jnp.where(valid[None, None, :], scores, LOW), axis=2).astype(jnp.bfloat16)
    context = jnp.einsum("hqk,khd->qhd", probs, value, preferred_element_type=jnp.float32)
    context = context.astype(jnp.bfloat16).reshape(rows, width)
    weight = lax.all_gather(out_weight, "ctx", axis=0, tiled=True)
    product = jnp.dot(context, weight, preferred_element_type=jnp.float32)
    return (stream.astype(jnp.float32) + product).astype(stream.dtype)


def local(query_frames, key_frames, value_frames, stream, out_weight):
    lanes, members = lax.axis_size("dp"), lax.axis_size("ctx")
    width, columns = out_weight.shape
    arguments = (query_frames, key_frames, value_frames, stream, out_weight)
    fits = width % HEAD_SIZE == 0 and columns % (lanes * HEAD_SIZE) == 0 and lanes & (lanes - 1) == 0
    if fits and members > 2 and lanes > 1:
        return by_slots(*arguments)
    return whole_window(*arguments)


def solution(mesh):
    in_specs = (
        P(("dp", "ctx"), None),
        P(("dp", "ctx"), None),
        P(("dp", "ctx"), None),
        P(("dp", "ctx"), None),
        P("ctx", None),
    )
    out_specs = P(("dp", "ctx"), None)
    return jax.shard_map(local, mesh=mesh, in_specs=in_specs, out_specs=out_specs, check_vma=False)
```

```python
import functools

import jax
import jax.numpy as jnp
from jax import lax
from jax.experimental import pallas as pl
from jax.experimental.pallas import tpu as pltpu
from jax.sharding import PartitionSpec as P

HEAD_SIZE = 128
LOG2_E = 1.4426950408889634
LOW = -1e30
MIB = 1024 * 1024
VMEM_MIB = 60
PAIR_SLOTS, MIDDLE_SLOTS = (4,), (4,)
LINE = 4
LANES = 8
VMEM = pl.BlockSpec(memory_space=pltpu.VMEM)
SMEM = pl.BlockSpec(memory_space=pltpu.SMEM)
ANY = pl.BlockSpec(memory_space=pl.ANY)
HAS_MIDDLE, GROUPS, SENT, OWNERS = 0, 1, 1 + LINE, 1 + 3 * LINE


def passed_along(value, steps):
    count = lax.axis_size("ctx")
    leading, last = (max(0, -steps), min(count, count - steps))
    return lax.ppermute(value, "ctx", [(source, source + steps) for source in range(leading, last)])


PAIR, ACROSS, OUTWARD = {0: 1, 1: 0, 2: 3, 3: 2}, {1: 2, 2: 1}, {1: 0, 2: 3}


def along_line(value, *ways):
    pairs = []
    for lane in range(LANES):
        for source, target in ways[lane % 2].items():
            pairs.append((lane * LINE + source, lane * LINE + target))
    return lax.ppermute(value, ("dp", "ctx"), pairs)


def in_plane(value, *masks):
    return lax.ppermute(value, "dp", [(lane, lane ^ masks[lane % 2]) for lane in range(LANES)])


def big_kernel():
    return pltpu.CompilerParams(vmem_limit_bytes=VMEM_MIB * MIB)


def no_cost():
    return pl.CostEstimate(flops=0, bytes_accessed=0, transcendentals=0)


def step(chain, tokens, operands=()):
    def kernel(*refs):
        del refs

    values = [chain, *operands]
    return pl.pallas_call(
        kernel,
        out_shape=[jax.ShapeDtypeStruct(value.shape, value.dtype) for value in values],
        in_specs=[ANY] * (len(values) + len(tokens)),
        out_specs=[ANY] * len(values),
        input_output_aliases={at: at for at in range(len(values))},
        cost_estimate=no_cost(),
        name="step",
    )(*values, *tokens)


CHIPS = ((0, 2, 4, 6), (0, 4, 2, 6))


def to_neighbours(piece):
    return in_plane(piece, 2, 4), in_plane(piece, 4, 2)


def to_diagonal(first):
    return in_plane(first, 4, 2)


def other_core(pieces):
    return [in_plane(piece, 1, 1) for piece in pieces]


def columns_of(group, width):
    return pl.ds(pl.multiple_of(group * width, HEAD_SIZE), width)


def pack_kernel(place, key_ref, value_ref, chain_ref, *out_refs):
    rows, width = key_ref.shape[0], key_ref.shape[1] // LINE
    chain_ref[...] = jnp.zeros_like(chain_ref)
    at = SENT
    for out_ref in out_refs:
        for column in range(0, out_ref.shape[1], width):
            columns = columns_of(place[at], width)
            out_ref[:rows, column : column + width] = key_ref[:, columns]
            out_ref[rows:, column : column + width] = value_ref[:, columns]
            at += 1


def packed(place, key_frames, value_frames, width, slots):
    rows = key_frames.shape[0]
    shapes = [jax.ShapeDtypeStruct((2 * rows, count * width), key_frames.dtype) for count in slots]
    shapes = [jax.ShapeDtypeStruct((8, HEAD_SIZE), jnp.float32)] + shapes
    whole = pl.BlockSpec(key_frames.shape, lambda at, place: (0, 0))
    return pl.pallas_call(
        pack_kernel,
        out_shape=shapes,
        grid_spec=pltpu.PrefetchScalarGridSpec(
            num_scalar_prefetch=1,
            grid=(1,),
            in_specs=[whole, whole],
            out_specs=[pl.BlockSpec(shape.shape, lambda at, place: (0, 0)) for shape in shapes],
        ),
        compiler_params=big_kernel(),
        cost_estimate=no_cost(),
        name="pack_window",
    )(place, key_frames, value_frames)


def attend(has_middle, query_ref, key_ref, value_ref, pair_ref, middle_ref, context_ref):
    rows, width = query_ref.shape
    ones = jnp.ones((rows, HEAD_SIZE), jnp.bfloat16)
    for at in range(0, width, HEAD_SIZE):
        head = pl.ds(at, HEAD_SIZE)
        query = query_ref[:, head]

        def scores(keys):
            return lax.dot_general(query, keys, (((1,), (1,)), ((), ())), preferred_element_type=jnp.float32)

        parts = [scores(key_ref[:, head]), scores(pair_ref[:rows, head])]
        parts.append(jnp.where(has_middle, scores(middle_ref[:rows, head]), LOW))
        values = [value_ref[:, head], pair_ref[rows:, head], middle_ref[rows:, head]]
        largest = jnp.max(functools.reduce(jnp.maximum, parts), axis=1, keepdims=True)
        sums = 0.0
        for part, value in zip(parts, values):
            expon = jnp.exp2((part - largest) * (HEAD_SIZE ** (-0.5) * LOG2_E)).astype(jnp.bfloat16)
            sums += jnp.dot(expon, jnp.concatenate([value, ones], 1), preferred_element_type=jnp.float32)
        context_ref[:, head] = (sums[:, :HEAD_SIZE] / sums[:, HEAD_SIZE:]).astype(context_ref.dtype)


def slots_kernel(slots, side_at, counts, place, query_ref, key_ref, value_ref, base_ref, *refs):
    refs = list(refs)
    sides = [[refs.pop(0), refs.pop(0)] for _ in slots]
    weights = [[refs.pop(0) for _ in range(count)] for count in counts]
    out_ref, own, beside, held, base, done, context, own_sems, held_sems, block_sems = refs
    depth, width = own.shape[3], held.shape[2]
    columns = [columns_of(place[OWNERS + at], width) for at in range(LANES)]

    def begin(source, target, sem):
        copy = pltpu.make_async_copy(source, target, sem)
        copy.start()
        return copy

    def begin_block(nth):
        found = [begin(base_ref.at[:, columns[nth]], base.at[nth], block_sems.at[0, nth])]
        for at, weight in enumerate(weights):
            owner = place[OWNERS + nth]
            if len(weight) == LANES:
                part = weight[nth]
            elif weight[0].shape[0] == depth:
                part = weight[0].at[:, columns[nth]]
            else:
                part = weight[0].at[pl.ds(pl.multiple_of(owner * depth, depth), depth)]
            found.append(begin(part, held.at[nth, pl.ds(at * depth, depth)], held_sems.at[at, nth]))
        return found

    frames = []
    for at, slot in enumerate(slots):
        group = columns_of(place[GROUPS + slot], depth)
        found = []
        for nth, ref in enumerate((query_ref, key_ref, value_ref)):
            found.append(begin(ref.at[:, group], own.at[at, nth], own_sems.at[at, nth]))
        for nth, ref in enumerate(sides[at]):
            part = ref.at[:, pl.ds(side_at[at][nth] * depth, depth)]
            found.append(begin(part, beside.at[at, nth], own_sems.at[at, 3 + nth]))
        frames.append(found)
    blocks = []
    for at in range(len(slots)):
        for copy in frames[at]:
            copy.wait()
        if at == 0:
            blocks += [begin_block(nth) for nth in range(LANES // 2)]
        part = context.at[:, pl.ds(at * depth, depth)]
        attend(place[HAS_MIDDLE] > 0, *(own.at[at, nth] for nth in range(3)), beside.at[at, 0], beside.at[at, 1], part)
        if at == 0:
            blocks += [begin_block(nth) for nth in range(LANES // 2, LANES)]
    leaving = []
    for nth in range(LANES):
        for copy in blocks[nth]:
            copy.wait()
        product = jnp.dot(context[...], held[nth], preferred_element_type=jnp.float32)
        done[nth] = (base[nth].astype(jnp.float32) + product).astype(done.dtype)
        leaving.append(begin(done.at[nth], out_ref.at[:, columns[nth]], block_sems.at[1, nth]))
    for copy in leaving:
        copy.wait()


def worked_off(slots, place, frames, base, sides, weights, dtype):
    rows, columns = base.shape
    depth, width = frames[0].shape[1] // LINE, columns // LANES
    count = len(slots)
    side_at = [[at for _, at in pair] for pair in sides]
    flat = [buffer for pair in sides for buffer, _ in pair] + [part for weight in weights for part in weight]
    kernel = functools.partial(slots_kernel, slots, side_at, [len(weight) for weight in weights])
    return pl.pallas_call(
        kernel,
        out_shape=jax.ShapeDtypeStruct(base.shape, dtype),
        in_specs=[SMEM] + [ANY] * (4 + len(flat)),
        out_specs=ANY,
        scratch_shapes=[
            pltpu.VMEM((count, 3, rows, depth), jnp.bfloat16),
            pltpu.VMEM((count, 2, 2 * rows, depth), jnp.bfloat16),
            pltpu.VMEM((LANES, count * depth, width), jnp.bfloat16),
            pltpu.VMEM((LANES, rows, width), base.dtype),
            pltpu.VMEM((LANES, rows, width), dtype),
            pltpu.VMEM((rows, count * depth), jnp.bfloat16),
            pltpu.SemaphoreType.DMA((count, 5)),
            pltpu.SemaphoreType.DMA((count, LANES)),
            pltpu.SemaphoreType.DMA((2, LANES)),
        ],
        compiler_params=big_kernel(),
        cost_estimate=pl.CostEstimate(
            flops=2 * rows * depth * count * (columns + 6 * rows),
            bytes_accessed=2 * depth * count * (columns + 7 * rows) + 8 * rows * columns,
            transcendentals=0,
        ),
        name="work_off_slots",
    )(place, *frames, base, *flat)


def by_slots(query_frames, key_frames, value_frames, stream, out_weight):
    width, columns = out_weight.shape
    position, lane = lax.axis_index("ctx"), lax.axis_index("dp")
    edge = (position == 0) | (position == LINE - 1)
    core = lane & 1

    def order(member):
        side = (member >= 2).astype(jnp.int32)
        return jnp.stack([member, member ^ 1, 2 - side, 3 - 3 * side])

    def by_core(one, other):
        return jnp.where(core == 0, one, other)

    to_pair, over_middle = order(position ^ 1), order(LINE - 1 - position)
    has_middle = 1 - edge.astype(jnp.int32)
    chips = by_core(jnp.array(CHIPS[0]), jnp.array(CHIPS[1]))
    other_chips = by_core(jnp.array(CHIPS[1]), jnp.array(CHIPS[0]))
    owners = [lane ^ chips, lane ^ 1 ^ other_chips]
    place = jnp.concatenate([has_middle[None], order(position), to_pair, over_middle, *owners]).astype(jnp.int32)

    share = columns // LANES
    mine = lax.dynamic_slice_in_dim(out_weight, lane * share, share, 1)
    slots = PAIR_SLOTS + MIDDLE_SLOTS
    chain, *packs = packed(place, key_frames, value_frames, width, slots)
    to_pair, over_middle = packs[: len(PAIR_SLOTS)], packs[len(PAIR_SLOTS) :]

    frames = (query_frames, key_frames, value_frames)

    def side(slot, buffers, counts):
        return [(buffer, at) for buffer, count in zip(buffers, counts) for at in range(count)][slot]

    def worked(slots, base, pairs, middles, weights, dtype):
        sides = [(side(slot, pairs, PAIR_SLOTS), side(slot, middles, MIDDLE_SLOTS)) for slot in slots]
        return worked_off(slots, place, frames, base, sides, weights, dtype)

    def to_pairs(value):
        return along_line(value, PAIR, PAIR)

    def to_middle(value):
        return along_line(value, ACROSS, ACROSS)

    first, crossed = to_pairs(mine), to_middle(mine)
    chain, first, crossed = step(chain, [], [first, crossed])
    outer, across = along_line(crossed, OUTWARD, OUTWARD), to_middle(first)
    first_near = to_neighbours(first)

    chain, *operands = step(chain, [], [*first_near, outer, across, *to_pair, *over_middle])
    first_near, (outer, across, *packs) = operands[:2], operands[2:]
    outer_next = along_line(across, OUTWARD, OUTWARD)
    pairs = [to_pairs(pack) for pack in packs[: len(to_pair)]]
    middles = [to_middle(pack) for pack in packs[len(to_pair) :]]
    first_all = [first, *first_near, to_diagonal(first_near[0])]
    second = jnp.where(edge, outer, crossed)
    second_near = to_neighbours(second)

    chain, outer_next, second, *operands = step(chain, [], [outer_next, second, *second_near, *first_all])
    second_near, first_all = operands[:2], operands[2:]
    third = jnp.where(edge, outer_next, across)
    third_near = to_neighbours(third)
    second_all = [second, *second_near, to_diagonal(second_near[0])]
    third_all = [third, *third_near, to_diagonal(third_near[0])]
    first_all += other_core(first_all)
    second_all += other_core(second_all)
    chain, third_all[3], *operands = step(chain, [], [third_all[3], *pairs, *middles])
    pairs, middles = operands[: len(pairs)], operands[len(pairs) :]
    third_all += other_core(third_all)

    weights = [[out_weight], first_all, second_all, third_all]
    return worked([0, 1, 2, 3], stream, pairs, middles, weights, stream.dtype)


def whole_window(query_frames, key_frames, value_frames, stream, out_weight):
    rows, width = query_frames.shape
    heads = width // HEAD_SIZE
    position, members = lax.axis_index("ctx"), lax.axis_size("ctx")
    both = jnp.stack([key_frames, value_frames], 0)
    window = jnp.concatenate([passed_along(both, 1), both, passed_along(both, -1)], 1)
    valid = jnp.repeat(jnp.stack([position > 0, True, position < members - 1]), rows)
    query, key, value = (a.reshape(-1, heads, HEAD_SIZE) for a in (query_frames, window[0], window[1]))
    scores = jnp.einsum("qhd,khd->hqk", query, key, preferred_element_type=jnp.float32) * HEAD_SIZE ** (-0.5)
    probs = jax.nn.softmax(jnp.where(valid[None, None, :], scores, LOW), axis=2).astype(jnp.bfloat16)
    context = jnp.einsum("hqk,khd->qhd", probs, value, preferred_element_type=jnp.float32)
    context = context.astype(jnp.bfloat16).reshape(rows, width)
    weight = lax.all_gather(out_weight, "ctx", axis=0, tiled=True)
    product = jnp.dot(context, weight, preferred_element_type=jnp.float32)
    return (stream.astype(jnp.float32) + product).astype(stream.dtype)


def local(query_frames, key_frames, value_frames, stream, out_weight):
    lanes, members = lax.axis_size("dp"), lax.axis_size("ctx")
    width, columns = out_weight.shape
    arguments = (query_frames, key_frames, value_frames, stream, out_weight)
    fits = width % HEAD_SIZE == 0 and columns % (lanes * HEAD_SIZE) == 0
    if fits and members == LINE and lanes == LANES:
        return by_slots(*arguments)
    return whole_window(*arguments)


def solution(mesh):
    in_specs = (
        P(("dp", "ctx"), None),
        P(("dp", "ctx"), None),
        P(("dp", "ctx"), None),
        P(("dp", "ctx"), None),
        P("ctx", None),
    )
    out_specs = P(("dp", "ctx"), None)
    return jax.shard_map(local, mesh=mesh, in_specs=in_specs, out_specs=out_specs, check_vma=False)
```

```python
import functools

import jax
import jax.numpy as jnp
from jax import lax
from jax.experimental import pallas as pl
from jax.experimental.pallas import tpu as pltpu
from jax.sharding import PartitionSpec as P

HEAD_SIZE = 128
LOG2_E = 1.4426950408889634
LOW = -1e30
MIB = 1024 * 1024
VMEM_MIB = 60
PAIR_SLOTS, MIDDLE_SLOTS = (3, 1), (3, 1)
LINE = 4
LANES = 8
VMEM = pl.BlockSpec(memory_space=pltpu.VMEM)
SMEM = pl.BlockSpec(memory_space=pltpu.SMEM)
ANY = pl.BlockSpec(memory_space=pl.ANY)
HAS_MIDDLE, GROUPS, SENT, OWNERS = 0, 1, 1 + LINE, 1 + 3 * LINE


def passed_along(value, steps):
    count = lax.axis_size("ctx")
    leading, last = (max(0, -steps), min(count, count - steps))
    return lax.ppermute(value, "ctx", [(source, source + steps) for source in range(leading, last)])


PAIR, ACROSS, OUTWARD = {0: 1, 1: 0, 2: 3, 3: 2}, {1: 2, 2: 1}, {1: 0, 2: 3}


def along_line(value, *ways):
    pairs = []
    for lane in range(LANES):
        for source, target in ways[lane % 2].items():
            pairs.append((lane * LINE + source, lane * LINE + target))
    return lax.ppermute(value, ("dp", "ctx"), pairs)


def in_plane(value, *masks):
    return lax.ppermute(value, "dp", [(lane, lane ^ masks[lane % 2]) for lane in range(LANES)])


def big_kernel():
    return pltpu.CompilerParams(vmem_limit_bytes=VMEM_MIB * MIB)


def no_cost():
    return pl.CostEstimate(flops=0, bytes_accessed=0, transcendentals=0)


def step(chain, tokens, operands=()):
    def kernel(*refs):
        del refs

    values = [chain, *operands]
    return pl.pallas_call(
        kernel,
        out_shape=[jax.ShapeDtypeStruct(value.shape, value.dtype) for value in values],
        in_specs=[ANY] * (len(values) + len(tokens)),
        out_specs=[ANY] * len(values),
        input_output_aliases={at: at for at in range(len(values))},
        cost_estimate=no_cost(),
        name="step",
    )(*values, *tokens)


CHIPS = ((0, 2, 4, 6), (0, 4, 2, 6))


def to_neighbours(piece):
    return in_plane(piece, 2, 4), in_plane(piece, 4, 2)


def to_diagonal(first):
    return in_plane(first, 4, 2)


def other_core(pieces):
    return [in_plane(piece, 1, 1) for piece in pieces]


def columns_of(group, width):
    return pl.ds(pl.multiple_of(group * width, HEAD_SIZE), width)


def pack_kernel(place, key_ref, value_ref, chain_ref, *out_refs):
    rows, width = key_ref.shape[0], key_ref.shape[1] // LINE
    chain_ref[...] = jnp.zeros_like(chain_ref)
    at = SENT
    for out_ref in out_refs:
        for column in range(0, out_ref.shape[1], width):
            columns = columns_of(place[at], width)
            out_ref[:rows, column : column + width] = key_ref[:, columns]
            out_ref[rows:, column : column + width] = value_ref[:, columns]
            at += 1


def packed(place, key_frames, value_frames, width, slots):
    rows = key_frames.shape[0]
    shapes = [jax.ShapeDtypeStruct((2 * rows, count * width), key_frames.dtype) for count in slots]
    shapes = [jax.ShapeDtypeStruct((8, HEAD_SIZE), jnp.float32)] + shapes
    whole = pl.BlockSpec(key_frames.shape, lambda at, place: (0, 0))
    return pl.pallas_call(
        pack_kernel,
        out_shape=shapes,
        grid_spec=pltpu.PrefetchScalarGridSpec(
            num_scalar_prefetch=1,
            grid=(1,),
            in_specs=[whole, whole],
            out_specs=[pl.BlockSpec(shape.shape, lambda at, place: (0, 0)) for shape in shapes],
        ),
        compiler_params=big_kernel(),
        cost_estimate=no_cost(),
        name="pack_window",
    )(place, key_frames, value_frames)


def attend(has_middle, query_ref, key_ref, value_ref, pair_ref, middle_ref, context_ref):
    rows, width = query_ref.shape
    ones = jnp.ones((rows, HEAD_SIZE), jnp.bfloat16)
    for at in range(0, width, HEAD_SIZE):
        head = pl.ds(at, HEAD_SIZE)
        query = query_ref[:, head]

        def scores(keys):
            return lax.dot_general(query, keys, (((1,), (1,)), ((), ())), preferred_element_type=jnp.float32)

        parts = [scores(key_ref[:, head]), scores(pair_ref[:rows, head])]
        parts.append(jnp.where(has_middle, scores(middle_ref[:rows, head]), LOW))
        values = [value_ref[:, head], pair_ref[rows:, head], middle_ref[rows:, head]]
        largest = jnp.max(functools.reduce(jnp.maximum, parts), axis=1, keepdims=True)
        sums = 0.0
        for part, value in zip(parts, values):
            expon = jnp.exp2((part - largest) * (HEAD_SIZE ** (-0.5) * LOG2_E)).astype(jnp.bfloat16)
            sums += jnp.dot(expon, jnp.concatenate([value, ones], 1), preferred_element_type=jnp.float32)
        context_ref[:, head] = (sums[:, :HEAD_SIZE] / sums[:, HEAD_SIZE:]).astype(context_ref.dtype)


def slots_kernel(slots, side_at, counts, place, query_ref, key_ref, value_ref, base_ref, *refs):
    refs = list(refs)
    sides = [[refs.pop(0), refs.pop(0)] for _ in slots]
    weights = [[refs.pop(0) for _ in range(count)] for count in counts]
    out_ref, own, beside, held, base, done, context, own_sems, held_sems, block_sems = refs
    depth, width = own.shape[3], held.shape[2]
    columns = [columns_of(place[OWNERS + at], width) for at in range(LANES)]

    def begin(source, target, sem):
        copy = pltpu.make_async_copy(source, target, sem)
        copy.start()
        return copy

    def begin_block(nth):
        found = [begin(base_ref.at[:, columns[nth]], base.at[nth], block_sems.at[0, nth])]
        for at, weight in enumerate(weights):
            owner = place[OWNERS + nth]
            if len(weight) == LANES:
                part = weight[nth]
            elif weight[0].shape[0] == depth:
                part = weight[0].at[:, columns[nth]]
            else:
                part = weight[0].at[pl.ds(pl.multiple_of(owner * depth, depth), depth)]
            found.append(begin(part, held.at[nth, pl.ds(at * depth, depth)], held_sems.at[at, nth]))
        return found

    frames = []
    for at, slot in enumerate(slots):
        group = columns_of(place[GROUPS + slot], depth)
        found = []
        for nth, ref in enumerate((query_ref, key_ref, value_ref)):
            found.append(begin(ref.at[:, group], own.at[at, nth], own_sems.at[at, nth]))
        for nth, ref in enumerate(sides[at]):
            part = ref.at[:, pl.ds(side_at[at][nth] * depth, depth)]
            found.append(begin(part, beside.at[at, nth], own_sems.at[at, 3 + nth]))
        frames.append(found)
    blocks = []
    for at in range(len(slots)):
        for copy in frames[at]:
            copy.wait()
        if at == 0:
            blocks += [begin_block(nth) for nth in range(LANES // 2)]
        part = context.at[:, pl.ds(at * depth, depth)]
        attend(place[HAS_MIDDLE] > 0, *(own.at[at, nth] for nth in range(3)), beside.at[at, 0], beside.at[at, 1], part)
        if at == 0:
            blocks += [begin_block(nth) for nth in range(LANES // 2, LANES)]
    leaving = []
    for nth in range(LANES):
        for copy in blocks[nth]:
            copy.wait()
        product = jnp.dot(context[...], held[nth], preferred_element_type=jnp.float32)
        done[nth] = (base[nth].astype(jnp.float32) + product).astype(done.dtype)
        leaving.append(begin(done.at[nth], out_ref.at[:, columns[nth]], block_sems.at[1, nth]))
    for copy in leaving:
        copy.wait()


def worked_off(slots, place, frames, base, sides, weights, dtype):
    rows, columns = base.shape
    depth, width = frames[0].shape[1] // LINE, columns // LANES
    count = len(slots)
    side_at = [[at for _, at in pair] for pair in sides]
    flat = [buffer for pair in sides for buffer, _ in pair] + [part for weight in weights for part in weight]
    kernel = functools.partial(slots_kernel, slots, side_at, [len(weight) for weight in weights])
    return pl.pallas_call(
        kernel,
        out_shape=jax.ShapeDtypeStruct(base.shape, dtype),
        in_specs=[SMEM] + [ANY] * (4 + len(flat)),
        out_specs=ANY,
        scratch_shapes=[
            pltpu.VMEM((count, 3, rows, depth), jnp.bfloat16),
            pltpu.VMEM((count, 2, 2 * rows, depth), jnp.bfloat16),
            pltpu.VMEM((LANES, count * depth, width), jnp.bfloat16),
            pltpu.VMEM((LANES, rows, width), base.dtype),
            pltpu.VMEM((LANES, rows, width), dtype),
            pltpu.VMEM((rows, count * depth), jnp.bfloat16),
            pltpu.SemaphoreType.DMA((count, 5)),
            pltpu.SemaphoreType.DMA((count, LANES)),
            pltpu.SemaphoreType.DMA((2, LANES)),
        ],
        compiler_params=big_kernel(),
        cost_estimate=pl.CostEstimate(
            flops=2 * rows * depth * count * (columns + 6 * rows),
            bytes_accessed=2 * depth * count * (columns + 7 * rows) + 8 * rows * columns,
            transcendentals=0,
        ),
        name="work_off_slots",
    )(place, *frames, base, *flat)


def by_slots(query_frames, key_frames, value_frames, stream, out_weight):
    width, columns = out_weight.shape
    position, lane = lax.axis_index("ctx"), lax.axis_index("dp")
    edge = (position == 0) | (position == LINE - 1)
    core = lane & 1

    def order(member):
        side = (member >= 2).astype(jnp.int32)
        return jnp.stack([member, member ^ 1, 2 - side, 3 - 3 * side])

    def by_core(one, other):
        return jnp.where(core == 0, one, other)

    to_pair, over_middle = order(position ^ 1), order(LINE - 1 - position)
    has_middle = 1 - edge.astype(jnp.int32)
    chips = by_core(jnp.array(CHIPS[0]), jnp.array(CHIPS[1]))
    other_chips = by_core(jnp.array(CHIPS[1]), jnp.array(CHIPS[0]))
    owners = [lane ^ chips, lane ^ 1 ^ other_chips]
    place = jnp.concatenate([has_middle[None], order(position), to_pair, over_middle, *owners]).astype(jnp.int32)

    share = columns // LANES
    mine = lax.dynamic_slice_in_dim(out_weight, lane * share, share, 1)
    slots = PAIR_SLOTS + MIDDLE_SLOTS
    chain, *packs = packed(place, key_frames, value_frames, width, slots)
    to_pair, over_middle = packs[: len(PAIR_SLOTS)], packs[len(PAIR_SLOTS) :]

    frames = (query_frames, key_frames, value_frames)

    def side(slot, buffers, counts):
        return [(buffer, at) for buffer, count in zip(buffers, counts) for at in range(count)][slot]

    def worked(slots, base, pairs, middles, weights, dtype):
        sides = [(side(slot, pairs, PAIR_SLOTS), side(slot, middles, MIDDLE_SLOTS)) for slot in slots]
        return worked_off(slots, place, frames, base, sides, weights, dtype)

    def to_pairs(value):
        return along_line(value, PAIR, PAIR)

    def to_middle(value):
        return along_line(value, ACROSS, ACROSS)

    first, crossed = to_pairs(mine), to_middle(mine)
    chain, first, crossed = step(chain, [], [first, crossed])
    outer, across = along_line(crossed, OUTWARD, OUTWARD), to_middle(first)
    first_near = to_neighbours(first)

    operands = [*first_near, outer, across, to_pair[0], over_middle[0]]
    chain, *operands = step(chain, [], operands)
    first_near, (outer, across, *packs) = operands[:2], operands[2:]
    outer_next = along_line(across, OUTWARD, OUTWARD)
    pairs, middles = [to_pairs(packs[0])], [to_middle(packs[1])]
    first_all = [first, *first_near, to_diagonal(first_near[0])]
    second = jnp.where(edge, outer, crossed)
    second_near = to_neighbours(second)

    operands = [outer_next, second, *second_near, *first_all]
    chain, *operands = step(chain, [], operands)
    outer_next, second, *operands = operands
    second_near, first_all = operands[:2], operands[2:]
    third = jnp.where(edge, outer_next, across)
    third_near = to_neighbours(third)
    second_all = [second, *second_near, to_diagonal(second_near[0])]
    third_all = [third, *third_near, to_diagonal(third_near[0])]
    first_all += other_core(first_all)
    operands = [pairs[0], middles[0], to_pair[1], over_middle[1], *second_all]
    chain, pairs[0], middles[0], pair_pack, pack, *second_all = step(chain, third_near, operands)
    pairs.append(to_pairs(pair_pack))
    middles.append(to_middle(pack))
    second_all += other_core(second_all)
    sums = worked([0, 1, 2], stream, pairs, middles, [[out_weight], first_all, second_all], jnp.float32)

    tokens = []
    chain, sums, pairs[1], middles[1], third_all[3] = step(chain, tokens, [sums, pairs[1], middles[1], third_all[3]])
    third_all += other_core(third_all)
    return worked([3], sums, pairs, middles, [third_all], stream.dtype)


def whole_window(query_frames, key_frames, value_frames, stream, out_weight):
    rows, width = query_frames.shape
    heads = width // HEAD_SIZE
    position, members = lax.axis_index("ctx"), lax.axis_size("ctx")
    both = jnp.stack([key_frames, value_frames], 0)
    window = jnp.concatenate([passed_along(both, 1), both, passed_along(both, -1)], 1)
    valid = jnp.repeat(jnp.stack([position > 0, True, position < members - 1]), rows)
    query, key, value = (a.reshape(-1, heads, HEAD_SIZE) for a in (query_frames, window[0], window[1]))
    scores = jnp.einsum("qhd,khd->hqk", query, key, preferred_element_type=jnp.float32) * HEAD_SIZE ** (-0.5)
    probs = jax.nn.softmax(jnp.where(valid[None, None, :], scores, LOW), axis=2).astype(jnp.bfloat16)
    context = jnp.einsum("hqk,khd->qhd", probs, value, preferred_element_type=jnp.float32)
    context = context.astype(jnp.bfloat16).reshape(rows, width)
    weight = lax.all_gather(out_weight, "ctx", axis=0, tiled=True)
    product = jnp.dot(context, weight, preferred_element_type=jnp.float32)
    return (stream.astype(jnp.float32) + product).astype(stream.dtype)


def local(query_frames, key_frames, value_frames, stream, out_weight):
    lanes, members = lax.axis_size("dp"), lax.axis_size("ctx")
    width, columns = out_weight.shape
    arguments = (query_frames, key_frames, value_frames, stream, out_weight)
    fits = width % HEAD_SIZE == 0 and columns % (lanes * HEAD_SIZE) == 0
    if fits and members == LINE and lanes == LANES:
        return by_slots(*arguments)
    return whole_window(*arguments)


def solution(mesh):
    in_specs = (
        P(("dp", "ctx"), None),
        P(("dp", "ctx"), None),
        P(("dp", "ctx"), None),
        P(("dp", "ctx"), None),
        P("ctx", None),
    )
    out_specs = P(("dp", "ctx"), None)
    return jax.shard_map(local, mesh=mesh, in_specs=in_specs, out_specs=out_specs, check_vma=False)
```

```python
import functools

import jax
import jax.numpy as jnp
from jax import lax
from jax.experimental import pallas as pl
from jax.experimental.pallas import tpu as pltpu
from jax.sharding import PartitionSpec as P

HEAD_SIZE = 128
LOG2_E = 1.4426950408889634
LOW = -1e30
MIB = 1024 * 1024
VMEM_MIB = 64
PAIR_SLOTS, MIDDLE_SLOTS = (3, 1), (4,)
LINE = 4
LANES = 8
VMEM = pl.BlockSpec(memory_space=pltpu.VMEM)
SMEM = pl.BlockSpec(memory_space=pltpu.SMEM)
ANY = pl.BlockSpec(memory_space=pl.ANY)
HAS_MIDDLE, GROUPS, SENT, OWNERS = 0, 1, 1 + LINE, 1 + 3 * LINE


def passed_along(value, steps):
    count = lax.axis_size("ctx")
    leading, last = (max(0, -steps), min(count, count - steps))
    return lax.ppermute(value, "ctx", [(source, source + steps) for source in range(leading, last)])


PAIR, ACROSS, OUTWARD = {0: 1, 1: 0, 2: 3, 3: 2}, {1: 2, 2: 1}, {1: 0, 2: 3}


def along_line(value, *ways):
    pairs = []
    for lane in range(LANES):
        for source, target in ways[lane % 2].items():
            pairs.append((lane * LINE + source, lane * LINE + target))
    return lax.ppermute(value, ("dp", "ctx"), pairs)


def in_plane(value, *masks):
    return lax.ppermute(value, "dp", [(lane, lane ^ masks[lane % 2]) for lane in range(LANES)])


def big_kernel():
    return pltpu.CompilerParams(vmem_limit_bytes=VMEM_MIB * MIB)


def no_cost():
    return pl.CostEstimate(flops=0, bytes_accessed=0, transcendentals=0)


def step(chain, tokens, operands=(), cost=0):
    def kernel(*refs):
        del refs

    values = [chain, *operands]
    return pl.pallas_call(
        kernel,
        out_shape=[jax.ShapeDtypeStruct(value.shape, value.dtype) for value in values],
        in_specs=[ANY] * (len(values) + len(tokens)),
        out_specs=[ANY] * len(values),
        input_output_aliases={at: at for at in range(len(values))},
        compiler_params=big_kernel(),
        cost_estimate=pl.CostEstimate(flops=0, bytes_accessed=cost, transcendentals=0),
        name="step",
    )(*values, *tokens)


CHIPS = ((0, 2, 4, 6), (0, 4, 2, 6))


def to_neighbours(piece):
    return in_plane(piece, 2, 4), in_plane(piece, 4, 2)


def to_diagonal(first):
    return in_plane(first, 4, 2)


def other_core(pieces):
    return [in_plane(piece, 1, 1) for piece in pieces]


def columns_of(group, width):
    return pl.ds(pl.multiple_of(group * width, HEAD_SIZE), width)


def pack_kernel(place, key_ref, value_ref, chain_ref, *out_refs):
    rows, width = key_ref.shape[0], key_ref.shape[1] // LINE
    chain_ref[...] = jnp.zeros_like(chain_ref)
    at = SENT
    for out_ref in out_refs:
        for column in range(0, out_ref.shape[1], width):
            columns = columns_of(place[at], width)
            out_ref[:rows, column : column + width] = key_ref[:, columns]
            out_ref[rows:, column : column + width] = value_ref[:, columns]
            at += 1


def packed(place, key_frames, value_frames, width, slots):
    rows = key_frames.shape[0]
    shapes = [jax.ShapeDtypeStruct((2 * rows, count * width), key_frames.dtype) for count in slots]
    shapes = [jax.ShapeDtypeStruct((8, HEAD_SIZE), jnp.float32)] + shapes
    whole = pl.BlockSpec(key_frames.shape, lambda at, place: (0, 0))
    return pl.pallas_call(
        pack_kernel,
        out_shape=shapes,
        grid_spec=pltpu.PrefetchScalarGridSpec(
            num_scalar_prefetch=1,
            grid=(1,),
            in_specs=[whole, whole],
            out_specs=[pl.BlockSpec(shape.shape, lambda at, place: (0, 0)) for shape in shapes],
        ),
        compiler_params=big_kernel(),
        cost_estimate=no_cost(),
        name="pack_window",
    )(place, key_frames, value_frames)


def attend(has_middle, query_ref, key_ref, value_ref, pair_ref, middle_ref, context_ref):
    rows, width = query_ref.shape
    ones = jnp.ones((rows, HEAD_SIZE), jnp.bfloat16)
    for at in range(0, width, HEAD_SIZE):
        head = pl.ds(at, HEAD_SIZE)
        query = query_ref[:, head]

        def scores(keys):
            return lax.dot_general(query, keys, (((1,), (1,)), ((), ())), preferred_element_type=jnp.float32)

        parts = [scores(key_ref[:, head]), scores(pair_ref[:rows, head])]
        parts.append(jnp.where(has_middle, scores(middle_ref[:rows, head]), LOW))
        values = [value_ref[:, head], pair_ref[rows:, head], middle_ref[rows:, head]]
        largest = jnp.max(functools.reduce(jnp.maximum, parts), axis=1, keepdims=True)
        sums = 0.0
        for part, value in zip(parts, values):
            expon = jnp.exp2((part - largest) * (HEAD_SIZE ** (-0.5) * LOG2_E)).astype(jnp.bfloat16)
            sums += jnp.dot(expon, jnp.concatenate([value, ones], 1), preferred_element_type=jnp.float32)
        context_ref[:, head] = (sums[:, :HEAD_SIZE] / sums[:, HEAD_SIZE:]).astype(context_ref.dtype)


def slots_kernel(slots, side_at, counts, place, query_ref, key_ref, value_ref, base_ref, *refs):
    refs = list(refs)
    sides = [[refs.pop(0), refs.pop(0)] for _ in slots]
    weights = [[refs.pop(0) for _ in range(count)] for count in counts]
    out_ref, own, beside, held, base, done, context, own_sems, held_sems, block_sems = refs
    depth, width = own.shape[3], held.shape[2]
    columns = [columns_of(place[OWNERS + at], width) for at in range(LANES)]

    def begin(source, target, sem):
        copy = pltpu.make_async_copy(source, target, sem)
        copy.start()
        return copy

    def begin_block(nth):
        found = [begin(base_ref.at[:, columns[nth]], base.at[nth], block_sems.at[0, nth])]
        for at, weight in enumerate(weights):
            owner = place[OWNERS + nth]
            if len(weight) == LANES:
                part = weight[nth]
            elif weight[0].shape[0] == depth:
                part = weight[0].at[:, columns[nth]]
            else:
                part = weight[0].at[pl.ds(pl.multiple_of(owner * depth, depth), depth)]
            found.append(begin(part, held.at[nth, pl.ds(at * depth, depth)], held_sems.at[at, nth]))
        return found

    frames = []
    for at, slot in enumerate(slots):
        group = columns_of(place[GROUPS + slot], depth)
        found = []
        for nth, ref in enumerate((query_ref, key_ref, value_ref)):
            found.append(begin(ref.at[:, group], own.at[at, nth], own_sems.at[at, nth]))
        for nth, ref in enumerate(sides[at]):
            part = ref.at[:, pl.ds(side_at[at][nth] * depth, depth)]
            found.append(begin(part, beside.at[at, nth], own_sems.at[at, 3 + nth]))
        frames.append(found)
    blocks = []
    for at in range(len(slots)):
        for copy in frames[at]:
            copy.wait()
        if at == 0:
            blocks += [begin_block(nth) for nth in range(LANES // 2)]
        part = context.at[:, pl.ds(at * depth, depth)]
        attend(place[HAS_MIDDLE] > 0, *(own.at[at, nth] for nth in range(3)), beside.at[at, 0], beside.at[at, 1], part)
        if at == 0:
            blocks += [begin_block(nth) for nth in range(LANES // 2, LANES)]
    leaving = []
    for nth in range(LANES):
        for copy in blocks[nth]:
            copy.wait()
        product = jnp.dot(context[...], held[nth], preferred_element_type=jnp.float32)
        done[nth] = (base[nth].astype(jnp.float32) + product).astype(done.dtype)
        leaving.append(begin(done.at[nth], out_ref.at[:, columns[nth]], block_sems.at[1, nth]))
    for copy in leaving:
        copy.wait()


def worked_off(slots, place, frames, base, sides, weights, dtype):
    rows, columns = base.shape
    depth, width = frames[0].shape[1] // LINE, columns // LANES
    count = len(slots)
    side_at = [[at for _, at in pair] for pair in sides]
    flat = [buffer for pair in sides for buffer, _ in pair] + [part for weight in weights for part in weight]
    kernel = functools.partial(slots_kernel, slots, side_at, [len(weight) for weight in weights])
    return pl.pallas_call(
        kernel,
        out_shape=jax.ShapeDtypeStruct(base.shape, dtype),
        in_specs=[SMEM] + [ANY] * (4 + len(flat)),
        out_specs=ANY,
        scratch_shapes=[
            pltpu.VMEM((count, 3, rows, depth), jnp.bfloat16),
            pltpu.VMEM((count, 2, 2 * rows, depth), jnp.bfloat16),
            pltpu.VMEM((LANES, count * depth, width), jnp.bfloat16),
            pltpu.VMEM((LANES, rows, width), base.dtype),
            pltpu.VMEM((LANES, rows, width), dtype),
            pltpu.VMEM((rows, count * depth), jnp.bfloat16),
            pltpu.SemaphoreType.DMA((count, 5)),
            pltpu.SemaphoreType.DMA((count, LANES)),
            pltpu.SemaphoreType.DMA((2, LANES)),
        ],
        compiler_params=big_kernel(),
        cost_estimate=pl.CostEstimate(
            flops=2 * rows * depth * count * (columns + 6 * rows),
            bytes_accessed=2 * depth * count * (columns + 7 * rows) + 8 * rows * columns,
            transcendentals=0,
        ),
        name="work_off_slots",
    )(place, *frames, base, *flat)


def by_slots(query_frames, key_frames, value_frames, stream, out_weight):
    width, columns = out_weight.shape
    position, lane = lax.axis_index("ctx"), lax.axis_index("dp")
    edge = (position == 0) | (position == LINE - 1)
    core = lane & 1

    def order(member):
        side = (member >= 2).astype(jnp.int32)
        return jnp.stack([member, member ^ 1, 2 - side, 3 - 3 * side])

    def by_core(one, other):
        return jnp.where(core == 0, one, other)

    to_pair, over_middle = order(position ^ 1), order(LINE - 1 - position)
    has_middle = 1 - edge.astype(jnp.int32)
    chips = by_core(jnp.array(CHIPS[0]), jnp.array(CHIPS[1]))
    other_chips = by_core(jnp.array(CHIPS[1]), jnp.array(CHIPS[0]))
    owners = [lane ^ chips, lane ^ 1 ^ other_chips]
    place = jnp.concatenate([has_middle[None], order(position), to_pair, over_middle, *owners]).astype(jnp.int32)

    share = columns // LANES
    mine = lax.dynamic_slice_in_dim(out_weight, lane * share, share, 1)
    slots = PAIR_SLOTS + MIDDLE_SLOTS
    chain, *packs = packed(place, key_frames, value_frames, width, slots)
    to_pair, over_middle = packs[: len(PAIR_SLOTS)], packs[len(PAIR_SLOTS) :]

    frames = (query_frames, key_frames, value_frames)

    def side(slot, buffers, counts):
        return [(buffer, at) for buffer, count in zip(buffers, counts) for at in range(count)][slot]

    def worked(slots, base, pairs, middles, weights, dtype):
        sides = [(side(slot, pairs, PAIR_SLOTS), side(slot, middles, MIDDLE_SLOTS)) for slot in slots]
        return worked_off(slots, place, frames, base, sides, weights, dtype)

    def to_pairs(value):
        return along_line(value, PAIR, PAIR)

    def to_middle(value):
        return along_line(value, ACROSS, ACROSS)

    first, crossed = to_pairs(mine), to_middle(mine)
    chain, first, crossed = step(chain, [], [first, crossed])
    outer, across = along_line(crossed, OUTWARD, OUTWARD), to_middle(first)
    first_near = to_neighbours(first)

    chain, outer, across, *packs = step(chain, [], [outer, across, to_pair[0], over_middle[0]])
    chain, *first_near = step(chain, [], first_near)
    outer_next = along_line(across, OUTWARD, OUTWARD)
    pairs, middles = [to_pairs(packs[0])], [to_middle(packs[1])]
    first_all = [first, *first_near, to_diagonal(first_near[0])]
    second = jnp.where(edge, outer, crossed)
    second_near = to_neighbours(second)

    chain, outer_next = step(chain, [], [outer_next])
    chain, second, *operands = step(chain, [], [second, *second_near, *first_all], 8 * MIB)
    second_near, first_all = operands[:2], operands[2:]
    third = jnp.where(edge, outer_next, across)
    third_near = to_neighbours(third)
    second_all = [second, *second_near, to_diagonal(second_near[0])]
    third_all = [third, *third_near, to_diagonal(third_near[0])]
    first_all += other_core(first_all)
    operands = [pairs[0], middles[0], to_pair[1], *second_all]
    chain, pairs[0], middles[0], pair_pack, *second_all = step(chain, third_near, operands)
    pairs.append(to_pairs(pair_pack))
    second_all += other_core(second_all)
    sums = worked([0, 1, 2], stream, pairs, middles, [[out_weight], first_all, second_all], jnp.float32)

    tokens = []
    chain, sums, pairs[1], third_all[3] = step(chain, tokens, [sums, pairs[1], third_all[3]])
    third_all += other_core(third_all)
    return worked([3], sums, pairs, middles, [third_all], stream.dtype)


def whole_window(query_frames, key_frames, value_frames, stream, out_weight):
    rows, width = query_frames.shape
    heads = width // HEAD_SIZE
    position, members = lax.axis_index("ctx"), lax.axis_size("ctx")
    both = jnp.stack([key_frames, value_frames], 0)
    window = jnp.concatenate([passed_along(both, 1), both, passed_along(both, -1)], 1)
    valid = jnp.repeat(jnp.stack([position > 0, True, position < members - 1]), rows)
    query, key, value = (a.reshape(-1, heads, HEAD_SIZE) for a in (query_frames, window[0], window[1]))
    scores = jnp.einsum("qhd,khd->hqk", query, key, preferred_element_type=jnp.float32) * HEAD_SIZE ** (-0.5)
    probs = jax.nn.softmax(jnp.where(valid[None, None, :], scores, LOW), axis=2).astype(jnp.bfloat16)
    context = jnp.einsum("hqk,khd->qhd", probs, value, preferred_element_type=jnp.float32)
    context = context.astype(jnp.bfloat16).reshape(rows, width)
    weight = lax.all_gather(out_weight, "ctx", axis=0, tiled=True)
    product = jnp.dot(context, weight, preferred_element_type=jnp.float32)
    return (stream.astype(jnp.float32) + product).astype(stream.dtype)


def local(query_frames, key_frames, value_frames, stream, out_weight):
    lanes, members = lax.axis_size("dp"), lax.axis_size("ctx")
    width, columns = out_weight.shape
    arguments = (query_frames, key_frames, value_frames, stream, out_weight)
    fits = width % HEAD_SIZE == 0 and columns % (lanes * HEAD_SIZE) == 0
    if fits and members == LINE and lanes == LANES:
        return by_slots(*arguments)
    return whole_window(*arguments)


def solution(mesh):
    in_specs = (
        P(("dp", "ctx"), None),
        P(("dp", "ctx"), None),
        P(("dp", "ctx"), None),
        P(("dp", "ctx"), None),
        P("ctx", None),
    )
    out_specs = P(("dp", "ctx"), None)
    return jax.shard_map(local, mesh=mesh, in_specs=in_specs, out_specs=out_specs, check_vma=False)
```

```python
import functools

import jax
import jax.numpy as jnp
from jax import lax
from jax.experimental import pallas as pl
from jax.experimental.pallas import tpu as pltpu
from jax.sharding import PartitionSpec as P

HEAD_SIZE = 128
LOG2_E = 1.4426950408889634
LOW = -1e30
MIB = 1024 * 1024
VMEM_MIB = 64
PAIR_SLOTS, MIDDLE_SLOTS = (3, 1), (4,)
LINE = 4
LANES = 8
VMEM = pl.BlockSpec(memory_space=pltpu.VMEM)
SMEM = pl.BlockSpec(memory_space=pltpu.SMEM)
ANY = pl.BlockSpec(memory_space=pl.ANY)
HAS_MIDDLE, GROUPS, SENT, OWNERS = 0, 1, 1 + LINE, 1 + 3 * LINE


def passed_along(value, steps):
    count = lax.axis_size("ctx")
    leading, last = (max(0, -steps), min(count, count - steps))
    return lax.ppermute(value, "ctx", [(source, source + steps) for source in range(leading, last)])


PAIR, ACROSS, OUTWARD = {0: 1, 1: 0, 2: 3, 3: 2}, {1: 2, 2: 1}, {1: 0, 2: 3}


def along_line(value, *ways):
    pairs = []
    for lane in range(LANES):
        for source, target in ways[lane % 2].items():
            pairs.append((lane * LINE + source, lane * LINE + target))
    return lax.ppermute(value, ("dp", "ctx"), pairs)


def in_plane(value, *masks):
    return lax.ppermute(value, "dp", [(lane, lane ^ masks[lane % 2]) for lane in range(LANES)])


def big_kernel():
    return pltpu.CompilerParams(vmem_limit_bytes=VMEM_MIB * MIB)


def no_cost():
    return pl.CostEstimate(flops=0, bytes_accessed=0, transcendentals=0)


def step(chain, tokens, operands=(), cost=0):
    def kernel(*refs):
        del refs

    values = [chain, *operands]
    return pl.pallas_call(
        kernel,
        out_shape=[jax.ShapeDtypeStruct(value.shape, value.dtype) for value in values],
        in_specs=[ANY] * (len(values) + len(tokens)),
        out_specs=[ANY] * len(values),
        input_output_aliases={at: at for at in range(len(values))},
        compiler_params=big_kernel(),
        cost_estimate=pl.CostEstimate(flops=0, bytes_accessed=cost, transcendentals=0),
        name="step",
    )(*values, *tokens)


CHIPS = ((0, 2, 4, 6), (0, 4, 2, 6))


def to_neighbours(piece):
    return in_plane(piece, 2, 4), in_plane(piece, 4, 2)


def to_diagonal(first):
    return in_plane(first, 4, 2)


def other_core(pieces):
    return [in_plane(piece, 1, 1) for piece in pieces]


def columns_of(group, width):
    return pl.ds(pl.multiple_of(group * width, HEAD_SIZE), width)


def pack_kernel(place, key_ref, value_ref, chain_ref, *out_refs):
    rows, width = key_ref.shape[0], key_ref.shape[1] // LINE
    chain_ref[...] = jnp.zeros_like(chain_ref)
    at = SENT
    for out_ref in out_refs:
        for column in range(0, out_ref.shape[1], width):
            columns = columns_of(place[at], width)
            out_ref[:rows, column : column + width] = key_ref[:, columns]
            out_ref[rows:, column : column + width] = value_ref[:, columns]
            at += 1


def packed(place, key_frames, value_frames, width, slots):
    rows = key_frames.shape[0]
    shapes = [jax.ShapeDtypeStruct((2 * rows, count * width), key_frames.dtype) for count in slots]
    shapes = [jax.ShapeDtypeStruct((8, HEAD_SIZE), jnp.float32)] + shapes
    whole = pl.BlockSpec(key_frames.shape, lambda at, place: (0, 0))
    return pl.pallas_call(
        pack_kernel,
        out_shape=shapes,
        grid_spec=pltpu.PrefetchScalarGridSpec(
            num_scalar_prefetch=1,
            grid=(1,),
            in_specs=[whole, whole],
            out_specs=[pl.BlockSpec(shape.shape, lambda at, place: (0, 0)) for shape in shapes],
        ),
        compiler_params=big_kernel(),
        cost_estimate=no_cost(),
        name="pack_window",
    )(place, key_frames, value_frames)


def attend(has_middle, query_ref, key_ref, value_ref, pair_ref, middle_ref, context_ref):
    rows, width = query_ref.shape
    ones = jnp.ones((rows, HEAD_SIZE), jnp.bfloat16)
    for at in range(0, width, HEAD_SIZE):
        head = pl.ds(at, HEAD_SIZE)
        query = query_ref[:, head]

        def scores(keys):
            return lax.dot_general(query, keys, (((1,), (1,)), ((), ())), preferred_element_type=jnp.float32)

        parts = [scores(key_ref[:, head]), scores(pair_ref[:rows, head])]
        parts.append(jnp.where(has_middle, scores(middle_ref[:rows, head]), LOW))
        values = [value_ref[:, head], pair_ref[rows:, head], middle_ref[rows:, head]]
        largest = jnp.max(functools.reduce(jnp.maximum, parts), axis=1, keepdims=True)
        sums = 0.0
        for part, value in zip(parts, values):
            expon = jnp.exp2((part - largest) * (HEAD_SIZE ** (-0.5) * LOG2_E)).astype(jnp.bfloat16)
            sums += jnp.dot(expon, jnp.concatenate([value, ones], 1), preferred_element_type=jnp.float32)
        context_ref[:, head] = (sums[:, :HEAD_SIZE] / sums[:, HEAD_SIZE:]).astype(context_ref.dtype)


def slots_kernel(slots, side_at, counts, place, query_ref, key_ref, value_ref, base_ref, *refs):
    refs = list(refs)
    sides = [[refs.pop(0), refs.pop(0)] for _ in slots]
    weights = [[refs.pop(0) for _ in range(count)] for count in counts]
    out_ref, own, beside, held, base, done, context, own_sems, held_sems, block_sems = refs
    depth, width = own.shape[3], held.shape[2]
    columns = [columns_of(place[OWNERS + at], width) for at in range(LANES)]

    def begin(source, target, sem):
        copy = pltpu.make_async_copy(source, target, sem)
        copy.start()
        return copy

    def begin_block(nth):
        found = [begin(base_ref.at[:, columns[nth]], base.at[nth], block_sems.at[0, nth])]
        for at, weight in enumerate(weights):
            owner = place[OWNERS + nth]
            if len(weight) == LANES:
                part = weight[nth]
            elif weight[0].shape[0] == depth:
                part = weight[0].at[:, columns[nth]]
            else:
                part = weight[0].at[pl.ds(pl.multiple_of(owner * depth, depth), depth)]
            found.append(begin(part, held.at[nth, pl.ds(at * depth, depth)], held_sems.at[at, nth]))
        return found

    frames = []
    for at, slot in enumerate(slots):
        group = columns_of(place[GROUPS + slot], depth)
        found = []
        for nth, ref in enumerate((query_ref, key_ref, value_ref)):
            found.append(begin(ref.at[:, group], own.at[at, nth], own_sems.at[at, nth]))
        for nth, ref in enumerate(sides[at]):
            part = ref.at[:, pl.ds(side_at[at][nth] * depth, depth)]
            found.append(begin(part, beside.at[at, nth], own_sems.at[at, 3 + nth]))
        frames.append(found)
    blocks, ahead = [], LANES // (len(slots) + 1)
    for at in range(len(slots)):
        for copy in frames[at]:
            copy.wait()
        if at == 0:
            blocks += [begin_block(nth) for nth in range(ahead)]
        part = context.at[:, pl.ds(at * depth, depth)]
        attend(place[HAS_MIDDLE] > 0, *(own.at[at, nth] for nth in range(3)), beside.at[at, 0], beside.at[at, 1], part)
        until = LANES if at == len(slots) - 1 else ahead * (at + 2)
        blocks += [begin_block(nth) for nth in range(len(blocks), until)]
    leaving = []
    for nth in range(LANES):
        for copy in blocks[nth]:
            copy.wait()
        product = jnp.dot(context[...], held[nth], preferred_element_type=jnp.float32)
        done[nth] = (base[nth].astype(jnp.float32) + product).astype(done.dtype)
        leaving.append(begin(done.at[nth], out_ref.at[:, columns[nth]], block_sems.at[1, nth]))
    for copy in leaving:
        copy.wait()


def worked_off(slots, place, frames, base, sides, weights, dtype):
    rows, columns = base.shape
    depth, width = frames[0].shape[1] // LINE, columns // LANES
    count = len(slots)
    side_at = [[at for _, at in pair] for pair in sides]
    flat = [buffer for pair in sides for buffer, _ in pair] + [part for weight in weights for part in weight]
    kernel = functools.partial(slots_kernel, slots, side_at, [len(weight) for weight in weights])
    return pl.pallas_call(
        kernel,
        out_shape=jax.ShapeDtypeStruct(base.shape, dtype),
        in_specs=[SMEM] + [ANY] * (4 + len(flat)),
        out_specs=ANY,
        scratch_shapes=[
            pltpu.VMEM((count, 3, rows, depth), jnp.bfloat16),
            pltpu.VMEM((count, 2, 2 * rows, depth), jnp.bfloat16),
            pltpu.VMEM((LANES, count * depth, width), jnp.bfloat16),
            pltpu.VMEM((LANES, rows, width), base.dtype),
            pltpu.VMEM((LANES, rows, width), dtype),
            pltpu.VMEM((rows, count * depth), jnp.bfloat16),
            pltpu.SemaphoreType.DMA((count, 5)),
            pltpu.SemaphoreType.DMA((count, LANES)),
            pltpu.SemaphoreType.DMA((2, LANES)),
        ],
        compiler_params=big_kernel(),
        cost_estimate=pl.CostEstimate(
            flops=2 * rows * depth * count * (columns + 6 * rows),
            bytes_accessed=2 * depth * count * (columns + 7 * rows) + 8 * rows * columns,
            transcendentals=0,
        ),
        name="work_off_slots",
    )(place, *frames, base, *flat)


def by_slots(query_frames, key_frames, value_frames, stream, out_weight):
    width, columns = out_weight.shape
    position, lane = lax.axis_index("ctx"), lax.axis_index("dp")
    edge = (position == 0) | (position == LINE - 1)
    core = lane & 1

    def order(member):
        side = (member >= 2).astype(jnp.int32)
        return jnp.stack([member, member ^ 1, 2 - side, 3 - 3 * side])

    def by_core(one, other):
        return jnp.where(core == 0, one, other)

    to_pair, over_middle = order(position ^ 1), order(LINE - 1 - position)
    has_middle = 1 - edge.astype(jnp.int32)
    chips = by_core(jnp.array(CHIPS[0]), jnp.array(CHIPS[1]))
    other_chips = by_core(jnp.array(CHIPS[1]), jnp.array(CHIPS[0]))
    owners = [lane ^ chips, lane ^ 1 ^ other_chips]
    place = jnp.concatenate([has_middle[None], order(position), to_pair, over_middle, *owners]).astype(jnp.int32)

    share = columns // LANES
    mine = lax.dynamic_slice_in_dim(out_weight, lane * share, share, 1)
    slots = PAIR_SLOTS + MIDDLE_SLOTS
    chain, *packs = packed(place, key_frames, value_frames, width, slots)
    to_pair, over_middle = packs[: len(PAIR_SLOTS)], packs[len(PAIR_SLOTS) :]

    frames = (query_frames, key_frames, value_frames)

    def side(slot, buffers, counts):
        return [(buffer, at) for buffer, count in zip(buffers, counts) for at in range(count)][slot]

    def worked(slots, base, pairs, middles, weights, dtype):
        sides = [(side(slot, pairs, PAIR_SLOTS), side(slot, middles, MIDDLE_SLOTS)) for slot in slots]
        return worked_off(slots, place, frames, base, sides, weights, dtype)

    def to_pairs(value):
        return along_line(value, PAIR, PAIR)

    def to_middle(value):
        return along_line(value, ACROSS, ACROSS)

    first, crossed = to_pairs(mine), to_middle(mine)
    chain, first, crossed = step(chain, [], [first, crossed])
    outer, across = along_line(crossed, OUTWARD, OUTWARD), to_middle(first)
    first_near = to_neighbours(first)

    chain, outer, across, *packs = step(chain, [], [outer, across, to_pair[0], over_middle[0]])
    chain, *first_near = step(chain, [], first_near)
    outer_next = along_line(across, OUTWARD, OUTWARD)
    pairs, middles = [to_pairs(packs[0])], [to_middle(packs[1])]
    first_all = [first, *first_near, to_diagonal(first_near[0])]
    second = jnp.where(edge, outer, crossed)
    second_near = to_neighbours(second)

    chain, outer_next = step(chain, [], [outer_next])
    chain, second, *operands = step(chain, [], [second, *second_near, *first_all], 8 * MIB)
    second_near, first_all = operands[:2], operands[2:]
    third = jnp.where(edge, outer_next, across)
    third_near = to_neighbours(third)
    second_all = [second, *second_near, to_diagonal(second_near[0])]
    third_all = [third, *third_near, to_diagonal(third_near[0])]
    first_all += other_core(first_all)
    operands = [pairs[0], middles[0], to_pair[1], second_all[3]]
    chain, pairs[0], middles[0], pair_pack, second_all[3] = step(chain, third_near, operands)
    pairs.append(to_pairs(pair_pack))
    second_all += other_core(second_all)
    sums = worked([0, 1, 2], stream, pairs, middles, [[out_weight], first_all, second_all], jnp.float32)

    tokens = []
    chain, sums, pairs[1], third_all[3] = step(chain, tokens, [sums, pairs[1], third_all[3]])
    third_all += other_core(third_all)
    return worked([3], sums, pairs, middles, [third_all], stream.dtype)


def whole_window(query_frames, key_frames, value_frames, stream, out_weight):
    rows, width = query_frames.shape
    heads = width // HEAD_SIZE
    position, members = lax.axis_index("ctx"), lax.axis_size("ctx")
    both = jnp.stack([key_frames, value_frames], 0)
    window = jnp.concatenate([passed_along(both, 1), both, passed_along(both, -1)], 1)
    valid = jnp.repeat(jnp.stack([position > 0, True, position < members - 1]), rows)
    query, key, value = (a.reshape(-1, heads, HEAD_SIZE) for a in (query_frames, window[0], window[1]))
    scores = jnp.einsum("qhd,khd->hqk", query, key, preferred_element_type=jnp.float32) * HEAD_SIZE ** (-0.5)
    probs = jax.nn.softmax(jnp.where(valid[None, None, :], scores, LOW), axis=2).astype(jnp.bfloat16)
    context = jnp.einsum("hqk,khd->qhd", probs, value, preferred_element_type=jnp.float32)
    context = context.astype(jnp.bfloat16).reshape(rows, width)
    weight = lax.all_gather(out_weight, "ctx", axis=0, tiled=True)
    product = jnp.dot(context, weight, preferred_element_type=jnp.float32)
    return (stream.astype(jnp.float32) + product).astype(stream.dtype)


def local(query_frames, key_frames, value_frames, stream, out_weight):
    lanes, members = lax.axis_size("dp"), lax.axis_size("ctx")
    width, columns = out_weight.shape
    arguments = (query_frames, key_frames, value_frames, stream, out_weight)
    fits = width % HEAD_SIZE == 0 and columns % (lanes * HEAD_SIZE) == 0
    if fits and members == LINE and lanes == LANES:
        return by_slots(*arguments)
    return whole_window(*arguments)


def solution(mesh):
    in_specs = (
        P(("dp", "ctx"), None),
        P(("dp", "ctx"), None),
        P(("dp", "ctx"), None),
        P(("dp", "ctx"), None),
        P("ctx", None),
    )
    out_specs = P(("dp", "ctx"), None)
    return jax.shard_map(local, mesh=mesh, in_specs=in_specs, out_specs=out_specs, check_vma=False)
```

```python
import functools

import jax
import jax.numpy as jnp
from jax import lax
from jax.experimental import pallas as pl
from jax.experimental.pallas import tpu as pltpu
from jax.sharding import PartitionSpec as P

HEAD_SIZE = 128
LOG2_E = 1.4426950408889634
LOW = -1e30
MIB = 1024 * 1024
VMEM_MIB = 64
PAIR_SLOTS, MIDDLE_SLOTS = (3, 1), (4,)
LINE = 4
LANES = 8
VMEM = pl.BlockSpec(memory_space=pltpu.VMEM)
SMEM = pl.BlockSpec(memory_space=pltpu.SMEM)
ANY = pl.BlockSpec(memory_space=pl.ANY)
HAS_MIDDLE, GROUPS, SENT, OWNERS = 0, 1, 1 + LINE, 1 + 3 * LINE


def passed_along(value, steps):
    count = lax.axis_size("ctx")
    leading, last = (max(0, -steps), min(count, count - steps))
    return lax.ppermute(value, "ctx", [(source, source + steps) for source in range(leading, last)])


PAIR, ACROSS, OUTWARD = {0: 1, 1: 0, 2: 3, 3: 2}, {1: 2, 2: 1}, {1: 0, 2: 3}


def along_line(value, *ways):
    pairs = []
    for lane in range(LANES):
        for source, target in ways[lane % 2].items():
            pairs.append((lane * LINE + source, lane * LINE + target))
    return lax.ppermute(value, ("dp", "ctx"), pairs)


def in_plane(value, *masks):
    return lax.ppermute(value, "dp", [(lane, lane ^ masks[lane % 2]) for lane in range(LANES)])


def big_kernel():
    return pltpu.CompilerParams(vmem_limit_bytes=VMEM_MIB * MIB)


def no_cost():
    return pl.CostEstimate(flops=0, bytes_accessed=0, transcendentals=0)


def step(chain, tokens, operands=(), cost=0):
    def kernel(*refs):
        del refs

    values = [chain, *operands]
    return pl.pallas_call(
        kernel,
        out_shape=[jax.ShapeDtypeStruct(value.shape, value.dtype) for value in values],
        in_specs=[ANY] * (len(values) + len(tokens)),
        out_specs=[ANY] * len(values),
        input_output_aliases={at: at for at in range(len(values))},
        compiler_params=big_kernel(),
        cost_estimate=pl.CostEstimate(flops=0, bytes_accessed=cost, transcendentals=0),
        name="step",
    )(*values, *tokens)


CHIPS = ((0, 2, 4, 6), (0, 4, 2, 6))


def to_neighbours(piece):
    return in_plane(piece, 2, 4), in_plane(piece, 4, 2)


def to_diagonal(first):
    return in_plane(first, 4, 2)


def other_core(pieces):
    return [in_plane(piece, 1, 1) for piece in pieces]


def columns_of(group, width):
    return pl.ds(pl.multiple_of(group * width, HEAD_SIZE), width)


def pack_kernel(place, key_ref, value_ref, chain_ref, *out_refs):
    rows, width = key_ref.shape[0], key_ref.shape[1] // LINE
    chain_ref[...] = jnp.zeros_like(chain_ref)
    at = SENT
    for out_ref in out_refs:
        for column in range(0, out_ref.shape[1], width):
            columns = columns_of(place[at], width)
            out_ref[:rows, column : column + width] = key_ref[:, columns]
            out_ref[rows:, column : column + width] = value_ref[:, columns]
            at += 1


def packed(place, key_frames, value_frames, width, slots):
    rows = key_frames.shape[0]
    shapes = [jax.ShapeDtypeStruct((2 * rows, count * width), key_frames.dtype) for count in slots]
    shapes = [jax.ShapeDtypeStruct((8, HEAD_SIZE), jnp.float32)] + shapes
    whole = pl.BlockSpec(key_frames.shape, lambda at, place: (0, 0))
    return pl.pallas_call(
        pack_kernel,
        out_shape=shapes,
        grid_spec=pltpu.PrefetchScalarGridSpec(
            num_scalar_prefetch=1,
            grid=(1,),
            in_specs=[whole, whole],
            out_specs=[pl.BlockSpec(shape.shape, lambda at, place: (0, 0)) for shape in shapes],
        ),
        compiler_params=big_kernel(),
        cost_estimate=no_cost(),
        name="pack_window",
    )(place, key_frames, value_frames)


def attend(has_middle, query_ref, key_ref, value_ref, pair_ref, middle_ref, context_ref):
    rows, width = query_ref.shape
    ones = jnp.ones((rows, HEAD_SIZE), jnp.bfloat16)
    for at in range(0, width, HEAD_SIZE):
        head = pl.ds(at, HEAD_SIZE)
        query = query_ref[:, head]

        def scores(keys):
            return lax.dot_general(query, keys, (((1,), (1,)), ((), ())), preferred_element_type=jnp.float32)

        parts = [scores(key_ref[:, head]), scores(pair_ref[:rows, head])]
        parts.append(jnp.where(has_middle, scores(middle_ref[:rows, head]), LOW))
        values = [value_ref[:, head], pair_ref[rows:, head], middle_ref[rows:, head]]
        largest = jnp.max(functools.reduce(jnp.maximum, parts), axis=1, keepdims=True)
        sums = 0.0
        for part, value in zip(parts, values):
            expon = jnp.exp2((part - largest) * (HEAD_SIZE ** (-0.5) * LOG2_E)).astype(jnp.bfloat16)
            sums += jnp.dot(expon, jnp.concatenate([value, ones], 1), preferred_element_type=jnp.float32)
        context_ref[:, head] = (sums[:, :HEAD_SIZE] / sums[:, HEAD_SIZE:]).astype(context_ref.dtype)


def slots_kernel(slots, side_at, counts, place, query_ref, key_ref, value_ref, base_ref, *refs):
    refs = list(refs)
    sides = [[refs.pop(0), refs.pop(0)] for _ in slots]
    weights = [[refs.pop(0) for _ in range(count)] for count in counts]
    out_ref, own, beside, held, base, done, context, own_sems, held_sems, block_sems = refs
    depth, width = own.shape[3], held.shape[2]
    columns = [columns_of(place[OWNERS + at], width) for at in range(LANES)]

    def begin(source, target, sem):
        copy = pltpu.make_async_copy(source, target, sem)
        copy.start()
        return copy

    def begin_block(nth):
        found = [begin(base_ref.at[:, columns[nth]], base.at[nth], block_sems.at[0, nth])]
        for at, weight in enumerate(weights):
            owner = place[OWNERS + nth]
            if len(weight) == LANES:
                part = weight[nth]
            elif weight[0].shape[0] == depth:
                part = weight[0].at[:, columns[nth]]
            else:
                part = weight[0].at[pl.ds(pl.multiple_of(owner * depth, depth), depth)]
            found.append(begin(part, held.at[nth, pl.ds(at * depth, depth)], held_sems.at[at, nth]))
        return found

    frames = []
    for at, slot in enumerate(slots):
        group = columns_of(place[GROUPS + slot], depth)
        found = []
        for nth, ref in enumerate((query_ref, key_ref, value_ref)):
            found.append(begin(ref.at[:, group], own.at[at, nth], own_sems.at[at, nth]))
        for nth, ref in enumerate(sides[at]):
            part = ref.at[:, pl.ds(side_at[at][nth] * depth, depth)]
            found.append(begin(part, beside.at[at, nth], own_sems.at[at, 3 + nth]))
        frames.append(found)
    blocks, ahead = [], 3 if len(slots) > 1 else LANES // 2
    for at in range(len(slots)):
        for copy in frames[at]:
            copy.wait()
        if at == 0:
            blocks += [begin_block(nth) for nth in range(ahead)]
        part = context.at[:, pl.ds(at * depth, depth)]
        attend(place[HAS_MIDDLE] > 0, *(own.at[at, nth] for nth in range(3)), beside.at[at, 0], beside.at[at, 1], part)
        until = LANES if at == len(slots) - 1 else min(LANES, ahead * (at + 2))
        blocks += [begin_block(nth) for nth in range(len(blocks), until)]
    leaving = []
    for nth in range(LANES):
        for copy in blocks[nth]:
            copy.wait()
        product = jnp.dot(context[...], held[nth], preferred_element_type=jnp.float32)
        done[nth] = (base[nth].astype(jnp.float32) + product).astype(done.dtype)
        leaving.append(begin(done.at[nth], out_ref.at[:, columns[nth]], block_sems.at[1, nth]))
    for copy in leaving:
        copy.wait()


def worked_off(slots, place, frames, base, sides, weights, dtype):
    rows, columns = base.shape
    depth, width = frames[0].shape[1] // LINE, columns // LANES
    count = len(slots)
    side_at = [[at for _, at in pair] for pair in sides]
    flat = [buffer for pair in sides for buffer, _ in pair] + [part for weight in weights for part in weight]
    kernel = functools.partial(slots_kernel, slots, side_at, [len(weight) for weight in weights])
    return pl.pallas_call(
        kernel,
        out_shape=jax.ShapeDtypeStruct(base.shape, dtype),
        in_specs=[SMEM] + [ANY] * (4 + len(flat)),
        out_specs=ANY,
        scratch_shapes=[
            pltpu.VMEM((count, 3, rows, depth), jnp.bfloat16),
            pltpu.VMEM((count, 2, 2 * rows, depth), jnp.bfloat16),
            pltpu.VMEM((LANES, count * depth, width), jnp.bfloat16),
            pltpu.VMEM((LANES, rows, width), base.dtype),
            pltpu.VMEM((LANES, rows, width), dtype),
            pltpu.VMEM((rows, count * depth), jnp.bfloat16),
            pltpu.SemaphoreType.DMA((count, 5)),
            pltpu.SemaphoreType.DMA((count, LANES)),
            pltpu.SemaphoreType.DMA((2, LANES)),
        ],
        compiler_params=big_kernel(),
        cost_estimate=pl.CostEstimate(
            flops=2 * rows * depth * count * (columns + 6 * rows),
            bytes_accessed=2 * depth * count * (columns + 7 * rows) + 8 * rows * columns,
            transcendentals=0,
        ),
        name="work_off_slots",
    )(place, *frames, base, *flat)


def by_slots(query_frames, key_frames, value_frames, stream, out_weight):
    width, columns = out_weight.shape
    position, lane = lax.axis_index("ctx"), lax.axis_index("dp")
    edge = (position == 0) | (position == LINE - 1)
    core = lane & 1

    def order(member):
        side = (member >= 2).astype(jnp.int32)
        return jnp.stack([member, member ^ 1, 2 - side, 3 - 3 * side])

    def by_core(one, other):
        return jnp.where(core == 0, one, other)

    to_pair, over_middle = order(position ^ 1), order(LINE - 1 - position)
    has_middle = 1 - edge.astype(jnp.int32)
    chips = by_core(jnp.array(CHIPS[0]), jnp.array(CHIPS[1]))
    other_chips = by_core(jnp.array(CHIPS[1]), jnp.array(CHIPS[0]))
    owners = [lane ^ chips, lane ^ 1 ^ other_chips]
    place = jnp.concatenate([has_middle[None], order(position), to_pair, over_middle, *owners]).astype(jnp.int32)

    share = columns // LANES
    mine = lax.dynamic_slice_in_dim(out_weight, lane * share, share, 1)
    slots = PAIR_SLOTS + MIDDLE_SLOTS
    chain, *packs = packed(place, key_frames, value_frames, width, slots)
    to_pair, over_middle = packs[: len(PAIR_SLOTS)], packs[len(PAIR_SLOTS) :]

    frames = (query_frames, key_frames, value_frames)

    def side(slot, buffers, counts):
        return [(buffer, at) for buffer, count in zip(buffers, counts) for at in range(count)][slot]

    def worked(slots, base, pairs, middles, weights, dtype):
        sides = [(side(slot, pairs, PAIR_SLOTS), side(slot, middles, MIDDLE_SLOTS)) for slot in slots]
        return worked_off(slots, place, frames, base, sides, weights, dtype)

    def to_pairs(value):
        return along_line(value, PAIR, PAIR)

    def to_middle(value):
        return along_line(value, ACROSS, ACROSS)

    first, crossed = to_pairs(mine), to_middle(mine)
    chain, first, crossed = step(chain, [], [first, crossed])
    outer, across = along_line(crossed, OUTWARD, OUTWARD), to_middle(first)
    first_near = to_neighbours(first)

    chain, outer, across, *packs = step(chain, [], [outer, across, to_pair[0], over_middle[0]])
    chain, *first_near = step(chain, [], first_near)
    outer_next = along_line(across, OUTWARD, OUTWARD)
    pairs, middles = [to_pairs(packs[0])], [to_middle(packs[1])]
    first_all = [first, *first_near, to_diagonal(first_near[0])]
    second = jnp.where(edge, outer, crossed)
    second_near = to_neighbours(second)

    chain, outer_next = step(chain, [], [outer_next])
    chain, second, *operands = step(chain, [], [second, *second_near, *first_all], 8 * MIB)
    second_near, first_all = operands[:2], operands[2:]
    third = jnp.where(edge, outer_next, across)
    third_near = to_neighbours(third)
    second_all = [second, *second_near, to_diagonal(second_near[0])]
    third_all = [third, *third_near, to_diagonal(third_near[0])]
    first_all += other_core(first_all)
    operands = [pairs[0], middles[0], to_pair[1], second_all[3]]
    chain, pairs[0], middles[0], pair_pack, second_all[3] = step(chain, third_near, operands)
    pairs.append(to_pairs(pair_pack))
    second_all += other_core(second_all)
    sums = worked([0, 1, 2], stream, pairs, middles, [[out_weight], first_all, second_all], jnp.float32)

    tokens = []
    chain, sums, pairs[1], third_all[3] = step(chain, tokens, [sums, pairs[1], third_all[3]])
    third_all += other_core(third_all)
    return worked([3], sums, pairs, middles, [third_all], stream.dtype)


def whole_window(query_frames, key_frames, value_frames, stream, out_weight):
    rows, width = query_frames.shape
    heads = width // HEAD_SIZE
    position, members = lax.axis_index("ctx"), lax.axis_size("ctx")
    both = jnp.stack([key_frames, value_frames], 0)
    window = jnp.concatenate([passed_along(both, 1), both, passed_along(both, -1)], 1)
    valid = jnp.repeat(jnp.stack([position > 0, True, position < members - 1]), rows)
    query, key, value = (a.reshape(-1, heads, HEAD_SIZE) for a in (query_frames, window[0], window[1]))
    scores = jnp.einsum("qhd,khd->hqk", query, key, preferred_element_type=jnp.float32) * HEAD_SIZE ** (-0.5)
    probs = jax.nn.softmax(jnp.where(valid[None, None, :], scores, LOW), axis=2).astype(jnp.bfloat16)
    context = jnp.einsum("hqk,khd->qhd", probs, value, preferred_element_type=jnp.float32)
    context = context.astype(jnp.bfloat16).reshape(rows, width)
    weight = lax.all_gather(out_weight, "ctx", axis=0, tiled=True)
    product = jnp.dot(context, weight, preferred_element_type=jnp.float32)
    return (stream.astype(jnp.float32) + product).astype(stream.dtype)


def local(query_frames, key_frames, value_frames, stream, out_weight):
    lanes, members = lax.axis_size("dp"), lax.axis_size("ctx")
    width, columns = out_weight.shape
    arguments = (query_frames, key_frames, value_frames, stream, out_weight)
    fits = width % HEAD_SIZE == 0 and columns % (lanes * HEAD_SIZE) == 0
    if fits and members == LINE and lanes == LANES:
        return by_slots(*arguments)
    return whole_window(*arguments)


def solution(mesh):
    in_specs = (
        P(("dp", "ctx"), None),
        P(("dp", "ctx"), None),
        P(("dp", "ctx"), None),
        P(("dp", "ctx"), None),
        P("ctx", None),
    )
    out_specs = P(("dp", "ctx"), None)
    return jax.shard_map(local, mesh=mesh, in_specs=in_specs, out_specs=out_specs, check_vma=False)
```

```python
import functools

import jax
import jax.numpy as jnp
from jax import lax
from jax.experimental import pallas as pl
from jax.experimental.pallas import tpu as pltpu
from jax.sharding import PartitionSpec as P

HEAD_SIZE = 128
LOG2_E = 1.4426950408889634
LOW = -1e30
MIB = 1024 * 1024
VMEM_MIB = 64
PAIR_SLOTS, MIDDLE_SLOTS = (3, 1), (4,)
LINE = 4
LANES = 8
VMEM = pl.BlockSpec(memory_space=pltpu.VMEM)
SMEM = pl.BlockSpec(memory_space=pltpu.SMEM)
ANY = pl.BlockSpec(memory_space=pl.ANY)
HAS_MIDDLE, GROUPS, SENT, OWNERS = 0, 1, 1 + LINE, 1 + 3 * LINE


def passed_along(value, steps):
    count = lax.axis_size("ctx")
    leading, last = (max(0, -steps), min(count, count - steps))
    return lax.ppermute(value, "ctx", [(source, source + steps) for source in range(leading, last)])


PAIR, ACROSS, OUTWARD = {0: 1, 1: 0, 2: 3, 3: 2}, {1: 2, 2: 1}, {1: 0, 2: 3}


def along_line(value, *ways):
    pairs = []
    for lane in range(LANES):
        for source, target in ways[lane % 2].items():
            pairs.append((lane * LINE + source, lane * LINE + target))
    return lax.ppermute(value, ("dp", "ctx"), pairs)


def in_plane(value, *masks):
    return lax.ppermute(value, "dp", [(lane, lane ^ masks[lane % 2]) for lane in range(LANES)])


def big_kernel():
    return pltpu.CompilerParams(vmem_limit_bytes=VMEM_MIB * MIB)


def no_cost():
    return pl.CostEstimate(flops=0, bytes_accessed=0, transcendentals=0)


def step(chain, tokens, operands=(), cost=0):
    def kernel(*refs):
        del refs

    values = [chain, *operands]
    return pl.pallas_call(
        kernel,
        out_shape=[jax.ShapeDtypeStruct(value.shape, value.dtype) for value in values],
        in_specs=[ANY] * (len(values) + len(tokens)),
        out_specs=[ANY] * len(values),
        input_output_aliases={at: at for at in range(len(values))},
        compiler_params=big_kernel(),
        cost_estimate=pl.CostEstimate(flops=0, bytes_accessed=cost, transcendentals=0),
        name="step",
    )(*values, *tokens)


CHIPS = ((0, 2, 4, 6), (0, 4, 2, 6))


def to_neighbours(piece):
    return in_plane(piece, 2, 4), in_plane(piece, 4, 2)


def to_diagonal(first):
    return in_plane(first, 4, 2)


def other_core(pieces):
    return [in_plane(piece, 1, 1) for piece in pieces]


def columns_of(group, width):
    return pl.ds(pl.multiple_of(group * width, HEAD_SIZE), width)


def pack_kernel(place, key_ref, value_ref, chain_ref, *out_refs):
    rows, width = key_ref.shape[0], key_ref.shape[1] // LINE
    chain_ref[...] = jnp.zeros_like(chain_ref)
    at = SENT
    for out_ref in out_refs:
        for column in range(0, out_ref.shape[1], width):
            columns = columns_of(place[at], width)
            out_ref[:rows, column : column + width] = key_ref[:, columns]
            out_ref[rows:, column : column + width] = value_ref[:, columns]
            at += 1


def packed(place, key_frames, value_frames, width, slots):
    rows = key_frames.shape[0]
    shapes = [jax.ShapeDtypeStruct((2 * rows, count * width), key_frames.dtype) for count in slots]
    shapes = [jax.ShapeDtypeStruct((8, HEAD_SIZE), jnp.float32)] + shapes
    whole = pl.BlockSpec(key_frames.shape, lambda at, place: (0, 0))
    return pl.pallas_call(
        pack_kernel,
        out_shape=shapes,
        grid_spec=pltpu.PrefetchScalarGridSpec(
            num_scalar_prefetch=1,
            grid=(1,),
            in_specs=[whole, whole],
            out_specs=[pl.BlockSpec(shape.shape, lambda at, place: (0, 0)) for shape in shapes],
        ),
        compiler_params=big_kernel(),
        cost_estimate=no_cost(),
        name="pack_window",
    )(place, key_frames, value_frames)


def attend(has_middle, query_ref, key_ref, value_ref, pair_ref, middle_ref, context_ref):
    rows, width = query_ref.shape
    ones = jnp.ones((rows, HEAD_SIZE), jnp.bfloat16)
    for at in range(0, width, HEAD_SIZE):
        head = pl.ds(at, HEAD_SIZE)
        query = query_ref[:, head]

        def scores(keys):
            return lax.dot_general(query, keys, (((1,), (1,)), ((), ())), preferred_element_type=jnp.float32)

        parts = [scores(key_ref[:, head]), scores(pair_ref[:rows, head])]
        parts.append(jnp.where(has_middle, scores(middle_ref[:rows, head]), LOW))
        values = [value_ref[:, head], pair_ref[rows:, head], middle_ref[rows:, head]]
        largest = jnp.max(functools.reduce(jnp.maximum, parts), axis=1, keepdims=True)
        sums = 0.0
        for part, value in zip(parts, values):
            expon = jnp.exp2((part - largest) * (HEAD_SIZE ** (-0.5) * LOG2_E)).astype(jnp.bfloat16)
            sums += jnp.dot(expon, jnp.concatenate([value, ones], 1), preferred_element_type=jnp.float32)
        context_ref[:, head] = (sums[:, :HEAD_SIZE] / sums[:, HEAD_SIZE:]).astype(context_ref.dtype)


def slots_kernel(slots, side_at, counts, place, query_ref, key_ref, value_ref, base_ref, *refs):
    refs = list(refs)
    sides = [[refs.pop(0), refs.pop(0)] for _ in slots]
    weights = [[refs.pop(0) for _ in range(count)] for count in counts]
    out_ref, own, beside, held, base, done, context, own_sems, held_sems, block_sems = refs
    depth, width = own.shape[3], held.shape[2]
    columns = [columns_of(place[OWNERS + at], width) for at in range(LANES)]

    def begin(source, target, sem):
        copy = pltpu.make_async_copy(source, target, sem)
        copy.start()
        return copy

    def begin_block(nth):
        found = [begin(base_ref.at[:, columns[nth]], base.at[nth], block_sems.at[0, nth])]
        for at, weight in enumerate(weights):
            owner = place[OWNERS + nth]
            if len(weight) == LANES:
                part = weight[nth]
            elif weight[0].shape[0] == depth:
                part = weight[0].at[:, columns[nth]]
            else:
                part = weight[0].at[pl.ds(pl.multiple_of(owner * depth, depth), depth)]
            found.append(begin(part, held.at[nth, pl.ds(at * depth, depth)], held_sems.at[at, nth]))
        return found

    frames = []
    for at, slot in enumerate(slots):
        group = columns_of(place[GROUPS + slot], depth)
        found = []
        for nth, ref in enumerate((query_ref, key_ref, value_ref)):
            found.append(begin(ref.at[:, group], own.at[at, nth], own_sems.at[at, nth]))
        for nth, ref in enumerate(sides[at]):
            part = ref.at[:, pl.ds(side_at[at][nth] * depth, depth)]
            found.append(begin(part, beside.at[at, nth], own_sems.at[at, 3 + nth]))
        frames.append(found)
    blocks, ahead = [], 3 if len(slots) > 1 else LANES // 2
    for at in range(len(slots)):
        for copy in frames[at]:
            copy.wait()
        if at == 0:
            blocks += [begin_block(nth) for nth in range(ahead)]
        part = context.at[:, pl.ds(at * depth, depth)]
        attend(place[HAS_MIDDLE] > 0, *(own.at[at, nth] for nth in range(3)), beside.at[at, 0], beside.at[at, 1], part)
        until = LANES if at == len(slots) - 1 else min(LANES, ahead * (at + 2))
        blocks += [begin_block(nth) for nth in range(len(blocks), until)]
    leaving = []
    for nth in range(LANES):
        for copy in blocks[nth]:
            copy.wait()
        product = jnp.dot(context[...], held[nth], preferred_element_type=jnp.float32)
        done[nth] = (base[nth].astype(jnp.float32) + product).astype(done.dtype)
        leaving.append(begin(done.at[nth], out_ref.at[:, columns[nth]], block_sems.at[1, nth]))
    for copy in leaving:
        copy.wait()


def worked_off(slots, place, frames, base, sides, weights, dtype):
    rows, columns = base.shape
    depth, width = frames[0].shape[1] // LINE, columns // LANES
    count = len(slots)
    side_at = [[at for _, at in pair] for pair in sides]
    flat = [buffer for pair in sides for buffer, _ in pair] + [part for weight in weights for part in weight]
    kernel = functools.partial(slots_kernel, slots, side_at, [len(weight) for weight in weights])
    return pl.pallas_call(
        kernel,
        out_shape=jax.ShapeDtypeStruct(base.shape, dtype),
        in_specs=[SMEM] + [ANY] * (4 + len(flat)),
        out_specs=ANY,
        scratch_shapes=[
            pltpu.VMEM((count, 3, rows, depth), jnp.bfloat16),
            pltpu.VMEM((count, 2, 2 * rows, depth), jnp.bfloat16),
            pltpu.VMEM((LANES, count * depth, width), jnp.bfloat16),
            pltpu.VMEM((LANES, rows, width), base.dtype),
            pltpu.VMEM((LANES, rows, width), dtype),
            pltpu.VMEM((rows, count * depth), jnp.bfloat16),
            pltpu.SemaphoreType.DMA((count, 5)),
            pltpu.SemaphoreType.DMA((count, LANES)),
            pltpu.SemaphoreType.DMA((2, LANES)),
        ],
        compiler_params=big_kernel(),
        cost_estimate=pl.CostEstimate(
            flops=2 * rows * depth * count * (columns + 6 * rows),
            bytes_accessed=2 * depth * count * (columns + 7 * rows) + 8 * rows * columns,
            transcendentals=0,
        ),
        name="work_off_slots",
    )(place, *frames, base, *flat)


def by_slots(query_frames, key_frames, value_frames, stream, out_weight):
    width, columns = out_weight.shape
    position, lane = lax.axis_index("ctx"), lax.axis_index("dp")
    edge = (position == 0) | (position == LINE - 1)
    core = lane & 1

    def order(member):
        side = (member >= 2).astype(jnp.int32)
        return jnp.stack([member, member ^ 1, 2 - side, 3 - 3 * side])

    def by_core(one, other):
        return jnp.where(core == 0, one, other)

    to_pair, over_middle = order(position ^ 1), order(LINE - 1 - position)
    has_middle = 1 - edge.astype(jnp.int32)
    chips = by_core(jnp.array(CHIPS[0]), jnp.array(CHIPS[1]))
    other_chips = by_core(jnp.array(CHIPS[1]), jnp.array(CHIPS[0]))
    owners = [lane ^ chips, lane ^ 1 ^ other_chips]
    place = jnp.concatenate([has_middle[None], order(position), to_pair, over_middle, *owners]).astype(jnp.int32)

    share = columns // LANES
    mine = lax.dynamic_slice_in_dim(out_weight, lane * share, share, 1)
    slots = PAIR_SLOTS + MIDDLE_SLOTS
    chain, *packs = packed(place, key_frames, value_frames, width, slots)
    to_pair, over_middle = packs[: len(PAIR_SLOTS)], packs[len(PAIR_SLOTS) :]

    frames = (query_frames, key_frames, value_frames)

    def side(slot, buffers, counts):
        return [(buffer, at) for buffer, count in zip(buffers, counts) for at in range(count)][slot]

    def worked(slots, base, pairs, middles, weights, dtype):
        sides = [(side(slot, pairs, PAIR_SLOTS), side(slot, middles, MIDDLE_SLOTS)) for slot in slots]
        return worked_off(slots, place, frames, base, sides, weights, dtype)

    def to_pairs(value):
        return along_line(value, PAIR, PAIR)

    def to_middle(value):
        return along_line(value, ACROSS, ACROSS)

    first, crossed = to_pairs(mine), to_middle(mine)
    chain, first, crossed = step(chain, [], [first, crossed])
    outer, across = along_line(crossed, OUTWARD, OUTWARD), to_middle(first)
    first_near = to_neighbours(first)

    chain, outer, across, *packs = step(chain, [], [outer, across, to_pair[0], over_middle[0]])
    chain, *first_near = step(chain, [], first_near)
    outer_next = along_line(across, OUTWARD, OUTWARD)
    pairs, middles = [to_pairs(packs[0])], [to_middle(packs[1])]
    first_all = [first, *first_near, to_diagonal(first_near[0])]
    second = jnp.where(edge, outer, crossed)
    second_near = to_neighbours(second)

    chain, outer_next = step(chain, [], [outer_next])
    chain, second, *operands = step(chain, [], [second, *second_near, *first_all], 24 * MIB)
    second_near, first_all = operands[:2], operands[2:]
    third = jnp.where(edge, outer_next, across)
    third_near = to_neighbours(third)
    second_all = [second, *second_near, to_diagonal(second_near[0])]
    third_all = [third, *third_near, to_diagonal(third_near[0])]
    first_all += other_core(first_all)
    operands = [pairs[0], middles[0], to_pair[1], second_all[3]]
    chain, pairs[0], middles[0], pair_pack, second_all[3] = step(chain, third_near, operands)
    pairs.append(to_pairs(pair_pack))
    second_all += other_core(second_all)
    sums = worked([0, 1, 2], stream, pairs, middles, [[out_weight], first_all, second_all], jnp.float32)

    tokens = []
    chain, sums, pairs[1], third_all[3] = step(chain, tokens, [sums, pairs[1], third_all[3]])
    third_all += other_core(third_all)
    return worked([3], sums, pairs, middles, [third_all], stream.dtype)


def whole_window(query_frames, key_frames, value_frames, stream, out_weight):
    rows, width = query_frames.shape
    heads = width // HEAD_SIZE
    position, members = lax.axis_index("ctx"), lax.axis_size("ctx")
    both = jnp.stack([key_frames, value_frames], 0)
    window = jnp.concatenate([passed_along(both, 1), both, passed_along(both, -1)], 1)
    valid = jnp.repeat(jnp.stack([position > 0, True, position < members - 1]), rows)
    query, key, value = (a.reshape(-1, heads, HEAD_SIZE) for a in (query_frames, window[0], window[1]))
    scores = jnp.einsum("qhd,khd->hqk", query, key, preferred_element_type=jnp.float32) * HEAD_SIZE ** (-0.5)
    probs = jax.nn.softmax(jnp.where(valid[None, None, :], scores, LOW), axis=2).astype(jnp.bfloat16)
    context = jnp.einsum("hqk,khd->qhd", probs, value, preferred_element_type=jnp.float32)
    context = context.astype(jnp.bfloat16).reshape(rows, width)
    weight = lax.all_gather(out_weight, "ctx", axis=0, tiled=True)
    product = jnp.dot(context, weight, preferred_element_type=jnp.float32)
    return (stream.astype(jnp.float32) + product).astype(stream.dtype)


def local(query_frames, key_frames, value_frames, stream, out_weight):
    lanes, members = lax.axis_size("dp"), lax.axis_size("ctx")
    width, columns = out_weight.shape
    arguments = (query_frames, key_frames, value_frames, stream, out_weight)
    fits = width % HEAD_SIZE == 0 and columns % (lanes * HEAD_SIZE) == 0
    if fits and members == LINE and lanes == LANES:
        return by_slots(*arguments)
    return whole_window(*arguments)


def solution(mesh):
    in_specs = (
        P(("dp", "ctx"), None),
        P(("dp", "ctx"), None),
        P(("dp", "ctx"), None),
        P(("dp", "ctx"), None),
        P("ctx", None),
    )
    out_specs = P(("dp", "ctx"), None)
    return jax.shard_map(local, mesh=mesh, in_specs=in_specs, out_specs=out_specs, check_vma=False)
```
